256 devices in a mesh: grid: 32 (over y, z_hi, core), orb: 8 (over x, z_lo).
Axes of the slice: x: 4, y: 4, z: 8 (z_hi: 4, z_lo: 2; z = z_hi * 2 + z_lo), core: 2. Of those that a mesh axis runs over, the one named last changes fastest.
Arguments:
- orbitals: bfloat16 [131072, 1024], P('grid', 'orb'), may hold values from -6 to 6
- potentials: bfloat16 [131072, 4096], P(('grid', 'orb')), may hold values from -0.0029296875 to 0.0029296875
- point_index: int32 [4096], replicated, may hold values from 0 to 131071, as said below
Outputs:
- exchange_applied: bfloat16 [131072, 1024], P('grid', 'orb')
The draws below stay inside these ranges and needn't reach their ends.
Inputs may be any that keep to these rules, and one draw needn't show every extreme that they name: `point_index`: the indices are distinct. Counting the grid points in aligned runs of 512, no run holds more than 32 interpolation points, and some run holds exactly 32.
All inputs are finite; a program needn't handle non-finite values.
Results may differ from the reference program's by a relative error of at most 0.005.
Values may be sent and summed in bfloat16 or wider, within the bound.
No kernel may reach another device: no remote copies, remote signals or barrier semaphores. Data moves between devices by JAX's collectives and lax.ppermute only.
A program may use at most 128 MiB of HBM per device.

```python
import jax
import jax.numpy as jnp
from jax import lax

NORB = 1024
NPTS = 4096
R_DEV = 512
NG = 131072
N_GRID = 32
N_ORB = 8


def draw_point_index(key, part):
    key = jax.random.fold_in(key, 7)
    devices = N_GRID * N_ORB
    average = NPTS // devices
    keys = jax.random.split(key, 5)
    pairs = devices // 2
    spread = jax.random.randint(keys[0], (pairs,), 0, average + 1)
    forced = jax.random.randint(keys[1], (), 0, pairs)
    spread = jnp.where(jnp.arange(pairs) == forced, average, spread)
    flipped = jax.random.randint(keys[2], (pairs,), 0, 2)
    first = average + spread * (1 - 2 * flipped)
    second = 2 * average - first
    counts = jnp.stack([first, second], 1).reshape(-1)
    ends = jnp.cumsum(counts)
    starts = ends - counts
    places = jnp.arange(NPTS)
    owners = jnp.searchsorted(ends, places, side='right')
    ranks = places - starts[owners]
    shuffled = jax.vmap(lambda inner: jax.random.permutation(inner, R_DEV))(jax.random.split(keys[3], devices))
    rows = owners * R_DEV + shuffled[owners, ranks]
    return rows[jax.random.permutation(keys[4], NPTS)].astype(jnp.int32)


def levels(own_key, extent, cuts, smallest, high):
    def one(position, blocks):
        steps = jax.random.uniform(jax.random.fold_in(jax.random.fold_in(own_key, 6), position), (blocks,), jnp.float32, smallest / len(cuts), high / len(cuts))
        return jnp.repeat(jnp.exp(steps), extent[position] // blocks).reshape((-1,) + (1,) * (len(extent) - position - 1))

    gain = one(*cuts[0])
    for cut in cuts[1:]:
        gain = gain * one(*cut)
    return gain


def bell_draw(key, shape, width, bound, pieces=(), dtype=jnp.bfloat16):
    loudness = levels(key, shape, pieces, -0.22, 0.18) if pieces else 1.0
    entries = jax.random.normal(key, shape, jnp.float32) * width * loudness
    return jnp.minimum(jnp.maximum(entries, -bound), bound).astype(dtype)


def setup_inputs(seed: int = 0) -> dict:
    arg_keys = jax.random.split(jax.random.key(seed), 4)
    orbitals = bell_draw(arg_keys[0], (NG, NORB), 1.0, 6.0, ((0, 32), (1, 8)))
    potentials = bell_draw(arg_keys[1], (NG, NPTS), ((NORB * NPTS) ** -0.5), 0.0029296875, ((0, 256),))
    point_index = draw_point_index(jax.random.fold_in(arg_keys[3], 71), 0)
    return {"orbitals": orbitals, "potentials": potentials, "point_index": point_index}


def reference(orbitals, potentials, point_index):
    point_values = jnp.take(orbitals, point_index, axis=0)
    blocks = NG // R_DEV
    orbital_blocks = orbitals.reshape(blocks, R_DEV, NORB)
    potential_blocks = potentials.reshape(blocks, R_DEV, NPTS)

    def one_block(pair):
        orbital_rows, potential_rows = pair
        density = jnp.dot(orbital_rows, point_values.T, preferred_element_type=jnp.float32)
        weighted = (potential_rows.astype(jnp.float32) * density).astype(jnp.bfloat16)
        applied = jnp.dot(weighted, point_values, preferred_element_type=jnp.float32)
        return (-applied).astype(jnp.bfloat16)

    result = lax.map(one_block, (orbital_blocks, potential_blocks))
    return result.reshape(NG, NORB)
```

```python
import jax
import jax.numpy as jnp
from jax import lax
from jax.experimental import pallas as pl
from jax.experimental.pallas import tpu as pltpu
from jax.sharding import PartitionSpec as P

NY, NZH, NC, NX, NZL = 4, 4, 2, 4, 2
AXES = ("grid", "orb")
BLOCK = 512


def moves(target):
    pairs = []
    for y in range(NY):
        for zh in range(NZH):
            for c in range(NC):
                for x in range(NX):
                    for zl in range(NZL):
                        ty, tzh, tc, tx, tzl = target(y, zh, c, x, zl)
                        src = ((y * NZH + zh) * NC + c) * NX * NZL + x * NZL + zl
                        dst = ((ty % NY * NZH + tzh % NZH) * NC + tc % NC) * NX * NZL + tx % NX * NZL + tzl % NZL
                        pairs.append((src, dst))
    return pairs


def send(value, target):
    return lax.ppermute(value, AXES, moves(target))


def to_core(value):
    return send(value, lambda y, zh, c, x, zl: (y, zh, 1 - c, x, zl))


def to_y(value, d):
    return send(value, lambda y, zh, c, x, zl: (y + d, zh, c, x, zl))


def to_zh(value, d):
    return send(value, lambda y, zh, c, x, zl: (y, zh + d, c, x, zl))


def to_zl(value):
    return send(value, lambda y, zh, c, x, zl: (y, zh, c, x, 1 - zl))


def first_axis(value, d):
    return send(value, lambda y, zh, c, x, zl: (y + d * c, zh, c, x + d * (1 - c), zl))


def second_axis(value, d):
    return send(value, lambda y, zh, c, x, zl: (y + d * (1 - c), zh, c, x + d * c, zl))


def pick_kernel(place, index, mine, other, *refs):
    outs, slot_ref = refs[:4], refs[4]
    slab, half, y = place[0], place[1], place[2]
    idx = index[...]
    owner = lax.shift_right_logical(idx, 12)
    in_mine = owner == slab
    in_other = owner == (slab ^ 1)
    flags = jnp.concatenate([in_mine.astype(jnp.float32), in_other.astype(jnp.float32)], axis=0)
    rows = lax.broadcasted_iota(jnp.int32, (BLOCK, BLOCK), 0)
    lanes = lax.broadcasted_iota(jnp.int32, (BLOCK, BLOCK), 1)
    upper = (rows <= lanes).astype(jnp.float32).astype(jnp.bfloat16)
    counts = jnp.dot(flags.astype(jnp.bfloat16), upper, preferred_element_type=jnp.float32)
    totals = counts[:, BLOCK - 1 : BLOCK]
    place_row = lax.broadcasted_iota(jnp.int32, (16, 1), 0)
    before = jnp.zeros((16, 1), jnp.float32)
    for i in range(16):
        last = 8 if i < 8 else 16
        later = (place_row > i) & (place_row < last)
        before = before + jnp.where(later, totals[i : i + 1, :], 0.0)
    ranks = counts + before - 1.0
    slot = jnp.where(in_mine, ranks[:8], jnp.where(in_other, ranks[8:] + 256.0, -1.0)).astype(jnp.int32)
    slot_ref[...] = slot
    local = idx & 4095
    high = lax.shift_right_logical(local, 6).astype(jnp.float32)
    low = (local & 63).astype(jnp.float32)
    where = jnp.zeros((BLOCK, 8), jnp.float32)
    pick_row = lax.broadcasted_iota(jnp.int32, (8, BLOCK), 0)
    for b in range(8):
        one_hot = (rows == slot[b : b + 1, :]).astype(jnp.float32).astype(jnp.bfloat16)
        parts = jnp.where(pick_row == 0, high[b : b + 1, :], jnp.where(pick_row == 1, low[b : b + 1, :], 0.0))
        where = where + lax.dot_general(
            one_hot, parts.astype(jnp.bfloat16), (((1,), (1,)), ((), ())), preferred_element_type=jnp.float32
        )
    line = (where[:, 0:1] * 64.0 + where[:, 1:2]).astype(jnp.int32)
    picked = []
    wide = 1024
    lane = lax.broadcasted_iota(jnp.int32, (256, wide), 1)
    for s, block in enumerate((mine, other)):
        want = line[s * 256 : (s + 1) * 256, :]
        total = jnp.zeros((256, 128), jnp.float32)
        for k in range(4096 // wide):
            one_hot = (want - k * wide == lane).astype(jnp.float32).astype(jnp.bfloat16)
            total = total + jnp.dot(one_hot, block[k * wide : (k + 1) * wide, :], preferred_element_type=jnp.float32)
        picked.append(total)
    turned = jnp.concatenate(picked, axis=0).T.astype(jnp.bfloat16)
    for d in range(4):
        b = half * 4 + lax.rem(y + d, 4)
        row = slot_ref[pl.ds(b, 1), :]
        one_hot = (rows == row).astype(jnp.float32).astype(jnp.bfloat16)
        outs[d][...] = jnp.dot(turned, one_hot, preferred_element_type=jnp.float32).astype(jnp.bfloat16)


def pick(place, index, mine, other):
    block = jax.ShapeDtypeStruct((128, BLOCK), jnp.bfloat16)
    vmem = pl.BlockSpec(memory_space=pltpu.VMEM)
    return pl.pallas_call(
        pick_kernel,
        out_shape=[block] * 4,
        in_specs=[pl.BlockSpec(memory_space=pltpu.SMEM), vmem, vmem, vmem],
        out_specs=[vmem] * 4,
        scratch_shapes=[pltpu.VMEM((8, BLOCK), jnp.int32)],
        compiler_params=pltpu.CompilerParams(vmem_limit_bytes=32 * 1024 * 1024),
        name="pick",
    )(place, index, mine, other)


def apply_kernel(place, rows_hbm, pot_hbm, *refs):
    mine, theirs = refs[0:4], refs[4:8]
    out = refs[8]
    points, rows, pots, acc, row_sem, pot_sem, point_sem = refs[9:]
    x, y, c = place[0], place[1], place[2]
    row_copies = [
        pltpu.make_async_copy(rows_hbm.at[o], rows.at[:, o * 128 : (o + 1) * 128], row_sem.at[o]) for o in range(8)
    ]
    for copy in row_copies:
        copy.start()

    def piece(arrays, k, i):
        if k < 4:
            source, block = arrays[k].at[i], lax.rem(x - i + 4, 4)
        else:
            source, block = arrays[i].at[k - 4], lax.rem(x - i + 4, 4)
        return pltpu.make_async_copy(
            source, points.at[k, pl.ds(pl.multiple_of(block * 256, 256), 256), :], point_sem.at[k, i]
        )

    def pot_copy(k):
        block = (k // 4) * 4 + lax.rem(y - k % 4 + 4, 4)
        return pltpu.make_async_copy(
            pot_hbm.at[:, pl.ds(pl.multiple_of(block * BLOCK, BLOCK), BLOCK)], pots.at[k], pot_sem.at[k]
        )

    for k in range(8):
        pot_copy(k).start()
        own = 0 if k < 4 else 1

        @pl.when(c == own)
        def _():
            for i in range(4):
                piece(mine, k, i).start()

        @pl.when(c != own)
        def _():
            for i in range(4):
                piece(theirs, k, i).start()

    for copy in row_copies:
        copy.wait()
    for k in range(8):
        pot_copy(k).wait()
        for i in range(4):
            piece(mine, k, i).wait()
        density = jnp.dot(rows[...], points[k], preferred_element_type=jnp.float32)
        weighted = (pots[k].astype(jnp.float32) * density).astype(jnp.bfloat16)
        part = lax.dot_general(
            weighted, points[k], (((1,), (1,)), ((), ())), preferred_element_type=jnp.float32
        )
        if k == 0:
            acc[...] = part
        elif k < 7:
            acc[...] += part
        else:
            total = -(acc[...] + part)
            for o in range(8):
                out[o] = total[:, o * 128 : (o + 1) * 128].astype(jnp.bfloat16)


def apply(place, rows_here, potentials, mine, theirs):
    anyspace = pl.BlockSpec(memory_space=pl.ANY)
    rows_each = potentials.shape[0]
    return pl.pallas_call(
        apply_kernel,
        out_shape=jax.ShapeDtypeStruct((8, rows_each, 128), jnp.bfloat16),
        in_specs=[pl.BlockSpec(memory_space=pltpu.SMEM)] + [anyspace] * 10,
        out_specs=pl.BlockSpec(memory_space=pltpu.VMEM),
        scratch_shapes=[
            pltpu.VMEM((8, 1024, BLOCK), jnp.bfloat16),
            pltpu.VMEM((rows_each, 1024), jnp.bfloat16),
            pltpu.VMEM((8, rows_each, BLOCK), jnp.bfloat16),
            pltpu.VMEM((rows_each, 1024), jnp.float32),
            pltpu.SemaphoreType.DMA((8,)),
            pltpu.SemaphoreType.DMA((8,)),
            pltpu.SemaphoreType.DMA((8, 4)),
        ],
        compiler_params=pltpu.CompilerParams(vmem_limit_bytes=40 * 1024 * 1024),
        cost_estimate=pl.CostEstimate(flops=4 * rows_each * 4096 * 1024, bytes_accessed=16 * 1024 * 1024, transcendentals=0),
        name="apply",
    )(place, rows_here, potentials, *mine, *theirs)


def shards(orbitals, potentials, point_index):
    grid, orb = lax.axis_index("grid"), lax.axis_index("orb")
    c = lax.rem(grid, NC)
    y = lax.div(grid, NZH * NC)
    x, zl = lax.div(orb, NZL), lax.rem(orb, NZL)
    pick_place = jnp.stack([grid, c, y]).astype(jnp.int32)
    apply_place = jnp.stack([x, y, c]).astype(jnp.int32)

    other = to_core(orbitals)
    rows_here = lax.all_to_all(orbitals.reshape(8, -1, 128), "orb", split_axis=0, concat_axis=0, tiled=True)
    blocks = pick(pick_place, point_index.reshape(8, BLOCK), orbitals, other)
    here = blocks[0] + to_y(blocks[1], 1) + to_y(blocks[3], 3) + to_y(blocks[2], 2)
    here = here + to_zh(here, 1) + to_zh(here, 3) + to_zh(here, 2)
    beside = to_zl(here)
    pair = jnp.where(zl == 0, jnp.concatenate([here, beside]), jnp.concatenate([beside, here]))
    line = jnp.stack([pair] + [first_axis(pair, d) for d in (1, 2, 3)])
    mine = [line] + [second_axis(line, d) for d in (1, 2, 3)]
    theirs = [to_core(value) for value in mine]
    result = apply(apply_place, rows_here, potentials, mine, theirs)
    return lax.all_to_all(result, "orb", split_axis=0, concat_axis=0, tiled=True).reshape(-1, 128)


def solution(mesh):
    return jax.shard_map(
        shards,
        mesh=mesh,
        in_specs=(P("grid", "orb"), P(("grid", "orb"), None), P()),
        out_specs=P("grid", "orb"),
        check_vma=False,
    )
```

```python
import functools

import jax
import jax.numpy as jnp
from jax import lax
from jax.experimental import pallas as pl
from jax.experimental.pallas import tpu as pltpu
from jax.sharding import PartitionSpec as P

NY, NZH, NC, NX, NZL = 4, 4, 2, 4, 2
AXES = ("grid", "orb")
BLOCK = 512
HALF = 256


def moves(target):
    pairs = []
    for y in range(NY):
        for zh in range(NZH):
            for c in range(NC):
                for x in range(NX):
                    for zl in range(NZL):
                        ty, tzh, tc, tx, tzl = target(y, zh, c, x, zl)
                        src = ((y * NZH + zh) * NC + c) * NX * NZL + x * NZL + zl
                        dst = ((ty % NY * NZH + tzh % NZH) * NC + tc % NC) * NX * NZL + tx % NX * NZL + tzl % NZL
                        pairs.append((src, dst))
    return pairs


def send(value, target):
    return lax.ppermute(value, AXES, moves(target))


def to_core(value):
    return send(value, lambda y, zh, c, x, zl: (y, zh, 1 - c, x, zl))


def to_y(value, d):
    return send(value, lambda y, zh, c, x, zl: (y + d, zh, c, x, zl))


def to_zh(value, d):
    return send(value, lambda y, zh, c, x, zl: (y, zh + d, c, x, zl))


def to_zl(value):
    return send(value, lambda y, zh, c, x, zl: (y, zh, c, x, 1 - zl))


def first_axis(value, d):
    return send(value, lambda y, zh, c, x, zl: (y + d * c, zh, c, x + d * (1 - c), zl))


def second_axis(value, d):
    return send(value, lambda y, zh, c, x, zl: (y + d * (1 - c), zh, c, x + d * c, zl))


def table_kernel(place, index, slot_ref, where_ref):
    slab = place[0]
    idx = index[...]
    lines = idx.shape[0]
    owner = lax.shift_right_logical(idx, 12)
    in_mine = owner == slab
    in_other = owner == (slab ^ 1)
    flags = jnp.concatenate([in_mine.astype(jnp.float32), in_other.astype(jnp.float32)], axis=0)
    upper = (
        (lax.broadcasted_iota(jnp.int32, (128, 128), 0) <= lax.broadcasted_iota(jnp.int32, (128, 128), 1))
        .astype(jnp.float32)
        .astype(jnp.bfloat16)
    )
    counts = jnp.dot(flags.astype(jnp.bfloat16), upper, preferred_element_type=jnp.float32)
    totals = jnp.broadcast_to(counts[:, 127:128], (2 * lines, 128)).astype(jnp.bfloat16)
    to = lax.broadcasted_iota(jnp.int32, (2 * lines, 2 * lines), 0)
    of = lax.broadcasted_iota(jnp.int32, (2 * lines, 2 * lines), 1)
    earlier = ((of < to) & ((of < lines) == (to < lines))).astype(jnp.float32).astype(jnp.bfloat16)
    ranks = counts + jnp.dot(earlier, totals, preferred_element_type=jnp.float32) - 1.0
    slot = jnp.where(in_mine, ranks[:lines], jnp.where(in_other, ranks[lines:] + 256.0, -1.0)).astype(jnp.int32)
    slot_ref[...] = slot
    local = idx & 4095
    high = lax.shift_right_logical(local, 6).astype(jnp.float32)
    low = (local & 63).astype(jnp.float32)
    where = jnp.zeros((BLOCK, 8), jnp.float32)
    rows = lax.broadcasted_iota(jnp.int32, (BLOCK, BLOCK), 0)
    pick_row = lax.broadcasted_iota(jnp.int32, (8, BLOCK), 0)

    def line(value, b):
        return jnp.concatenate([value[i : i + 1, :] for i in range(4 * b, 4 * b + 4)], axis=1)

    for b in range(8):
        one_hot = (rows == line(slot, b)).astype(jnp.float32).astype(jnp.bfloat16)
        parts = jnp.where(pick_row == 0, line(high, b), jnp.where(pick_row == 1, line(low, b), 0.0))
        where = where + lax.dot_general(
            one_hot, parts.astype(jnp.bfloat16), (((1,), (1,)), ((), ())), preferred_element_type=jnp.float32
        )
    where_ref[...] = where


def tables(place, index):
    vmem = pl.BlockSpec(memory_space=pltpu.VMEM)
    return pl.pallas_call(
        table_kernel,
        out_shape=[jax.ShapeDtypeStruct(index.shape, jnp.int32), jax.ShapeDtypeStruct((BLOCK, 8), jnp.float32)],
        in_specs=[pl.BlockSpec(memory_space=pltpu.SMEM), vmem],
        out_specs=[vmem] * 2,
        compiler_params=pltpu.CompilerParams(vmem_limit_bytes=16 * 1024 * 1024),
        name="tables",
    )(place, index)


def pick_kernel(place, slot_ref, where_ref, mine, other_hbm, *refs):
    outs, other, other_sem = refs[:4], refs[4], refs[5]
    other_copy = pltpu.make_async_copy(other_hbm, other, other_sem)
    other_copy.start()
    half, y = place[1], place[2]
    where = where_ref[...]
    line = (where[:, 0:1] * 64.0 + where[:, 1:2]).astype(jnp.int32)
    picked = []
    wide = 1024
    lane = lax.broadcasted_iota(jnp.int32, (256, wide), 1)
    for s, block in enumerate((mine, other)):
        if s == 1:
            other_copy.wait()
        want = line[s * 256 : (s + 1) * 256, :]
        total = jnp.zeros((256, 128), jnp.float32)
        for k in range(4096 // wide):
            one_hot = (want - k * wide == lane).astype(jnp.float32).astype(jnp.bfloat16)
            total = total + jnp.dot(one_hot, block[k * wide : (k + 1) * wide, :], preferred_element_type=jnp.float32)
        picked.append(total)
    turned = jnp.concatenate(picked, axis=0).T.astype(jnp.bfloat16)
    rows = lax.broadcasted_iota(jnp.int32, (BLOCK, BLOCK), 0)
    for d in range(4):
        b = half * 4 + lax.rem(y + d, 4)
        four = slot_ref[pl.ds(b * 4, 4), :]
        row = jnp.concatenate([four[i : i + 1, :] for i in range(4)], axis=1)
        one_hot = (rows == row).astype(jnp.float32).astype(jnp.bfloat16)
        values = jnp.dot(turned, one_hot, preferred_element_type=jnp.float32).astype(jnp.bfloat16)
        outs[d][0] = values[:, :HALF]
        outs[d][1] = values[:, HALF:]


def pick(place, slot, where, mine, other):
    block = jax.ShapeDtypeStruct((2, 128, HALF), jnp.bfloat16)
    vmem = pl.BlockSpec(memory_space=pltpu.VMEM)
    return pl.pallas_call(
        pick_kernel,
        out_shape=[block] * 4,
        in_specs=[pl.BlockSpec(memory_space=pltpu.SMEM), vmem, vmem, vmem, pl.BlockSpec(memory_space=pl.ANY)],
        out_specs=[vmem] * 4,
        scratch_shapes=[pltpu.VMEM(other.shape, other.dtype), pltpu.SemaphoreType.DMA],
        compiler_params=pltpu.CompilerParams(vmem_limit_bytes=16 * 1024 * 1024),
        name="pick",
    )(place, slot, where, mine, other)


def join_kernel(place, *refs):
    pieces, messages = refs[:4], refs[4:6]
    core = place[2]
    for c in range(2):

        @pl.when(core == c)
        def _():
            for d in range(4):
                for dz in range(2):
                    for half in range(2):
                        value = pieces[d][dz, half]
                        if c == 0:
                            messages[half][d, dz] = value
                        else:
                            messages[d // 2][d % 2 * 2 + half, dz] = value


def join(place, pieces):
    vmem = pl.BlockSpec(memory_space=pltpu.VMEM)
    message = jax.ShapeDtypeStruct((4, 2, 128, HALF), jnp.bfloat16)
    return pl.pallas_call(
        join_kernel,
        out_shape=[message] * 2,
        in_specs=[pl.BlockSpec(memory_space=pltpu.SMEM)] + [vmem] * 4,
        out_specs=[vmem] * 2,
        compiler_params=pltpu.CompilerParams(vmem_limit_bytes=16 * 1024 * 1024),
        name="join",
    )(place, *pieces)


def pack_kernel(place, *refs):
    core = place[2]
    sources, outs, sem = refs[:2], refs[2:4], refs[4]
    copies = []
    for s in range(2):
        for b in range(8):
            lanes = pl.ds(pl.multiple_of((core * 8 + b) * HALF, HALF), HALF)
            copies.append(pltpu.make_async_copy(sources[s].at[:, lanes], outs[s].at[b], sem.at[s, b]))
    for copy in copies:
        copy.start()
    for copy in copies:
        copy.wait()


def pack(place, mine, theirs):
    anyspace = pl.BlockSpec(memory_space=pl.ANY)
    return pl.pallas_call(
        pack_kernel,
        out_shape=[jax.ShapeDtypeStruct((8, mine.shape[0], HALF), jnp.bfloat16)] * 2,
        in_specs=[pl.BlockSpec(memory_space=pltpu.SMEM), anyspace, anyspace],
        out_specs=[pl.BlockSpec(memory_space=pltpu.VMEM)] * 2,
        scratch_shapes=[pltpu.SemaphoreType.DMA((2, 8))],
        compiler_params=pltpu.CompilerParams(vmem_limit_bytes=16 * 1024 * 1024),
        name="pack",
    )(place, mine, theirs)


def apply_kernel(half, sides, place, *refs):
    number = len(sides)
    row_refs, refs = refs[:number], refs[number:]
    pot_refs, refs = refs[:number], refs[number:]
    messages, refs = refs[:4], refs[4:]
    if half == 1:
        before, refs = refs[0], refs[1:]
    outs, (rows, weighted) = refs[:number], refs[number:]
    each = row_refs[0].shape[1]
    x, y, core, zl = place[0], place[1], place[2], place[3]

    def pot_block(k):
        first = lax.rem(y - k + 4, 4) * 2 + half
        second = lax.rem(y - (half * 2 + k // 2) + 4, 4) * 2 + k % 2
        return jnp.where(core == 0, first, second)

    for k in range(8):
        block = lax.rem(x - k // 2 + 4, 4) * 2 + (zl ^ (k % 2))
        for s in range(number):
            rows[s * each : (s + 1) * each, k * 128 : (k + 1) * 128] = row_refs[s][block]

    def work(c):
        for k in range(4):
            if c == 0:
                value = messages[k][...].reshape(1024, HALF)
            else:
                value = jnp.concatenate([messages[e][k].reshape(HALF, HALF) for e in range(4)], axis=0)
            density = jnp.dot(rows[...], value, preferred_element_type=jnp.float32)
            for s in range(number):
                part = slice(s * each, (s + 1) * each)
                pot = pot_refs[s][pot_block(k)].astype(jnp.float32)
                weighted[part, k * HALF : (k + 1) * HALF] = (pot * density[part]).astype(jnp.bfloat16)
        for n in range(4):
            lanes = slice(n * HALF, (n + 1) * HALF)
            if c == 0:
                parts = [messages[e][n].reshape(HALF, HALF) for e in range(4)]
            else:
                parts = [messages[n][k].reshape(HALF, HALF) for k in range(4)]
            total = lax.dot_general(
                weighted[...],
                jnp.concatenate(parts, axis=1),
                (((1,), (1,)), ((), ())),
                preferred_element_type=jnp.float32,
            )
            if half == 0:
                for s in range(number):
                    outs[s][:, lanes] = total[s * each : (s + 1) * each]
            else:
                outs[0][:, lanes] = (before[:, lanes] + total).astype(outs[0].dtype)

    for c in range(2):

        @pl.when(core == c)
        def _():
            work(c)


def apply(half, place, rows, pots, messages, before=None, dtype=jnp.float32):
    vmem = pl.BlockSpec(memory_space=pltpu.VMEM)
    number, each = len(rows), pots[0].shape[1]
    extra = [before] if half == 1 else []
    out = jax.ShapeDtypeStruct((each, 1024), dtype)
    return pl.pallas_call(
        functools.partial(apply_kernel, half, tuple(range(number))),
        out_shape=[out] * number,
        in_specs=[pl.BlockSpec(memory_space=pltpu.SMEM)]
        + [vmem] * (2 * number + 4 + len(extra)),
        out_specs=[vmem] * number,
        scratch_shapes=[
            pltpu.VMEM((number * each, 1024), jnp.bfloat16),
            pltpu.VMEM((number * each, 1024), jnp.bfloat16),
        ],
        compiler_params=pltpu.CompilerParams(vmem_limit_bytes=16 * 1024 * 1024),
        cost_estimate=pl.CostEstimate(
            flops=number * each * 4 * 1024 * 1024, bytes_accessed=number * 4 * 1024 * 1024, transcendentals=0
        ),
        name="apply_high" if half else "apply_low",
    )(place, *rows, *pots, *messages, *extra)


def total_kernel(place, mine, theirs, out):
    x, zl = place[0], place[3]
    for k in range(8):
        block = lax.rem(x - k // 2 + 4, 4) * 2 + (zl ^ (k % 2))
        lanes = slice(k * 128, (k + 1) * 128)
        out[block] = (-(mine[:, lanes] + theirs[:, lanes].astype(jnp.float32))).astype(jnp.bfloat16)


def total(place, mine, theirs):
    vmem = pl.BlockSpec(memory_space=pltpu.VMEM)
    return pl.pallas_call(
        total_kernel,
        out_shape=jax.ShapeDtypeStruct((8, mine.shape[0], 128), jnp.bfloat16),
        in_specs=[pl.BlockSpec(memory_space=pltpu.SMEM), vmem, vmem],
        out_specs=vmem,
        compiler_params=pltpu.CompilerParams(vmem_limit_bytes=16 * 1024 * 1024),
        name="total",
    )(place, mine, theirs)


def shards(orbitals, potentials, point_index):
    grid, orb = lax.axis_index("grid"), lax.axis_index("orb")
    c = lax.rem(grid, NC)
    y = lax.div(grid, NZH * NC)
    x, zl = lax.div(orb, NZL), lax.rem(orb, NZL)
    pick_place = jnp.stack([grid, c, y]).astype(jnp.int32)
    place = jnp.stack([x, y, c, zl]).astype(jnp.int32)

    other = to_core(orbitals)
    other_pot = to_core(potentials)
    rows_here = lax.all_to_all(orbitals.reshape(8, -1, 128), "orb", split_axis=0, concat_axis=0, tiled=True)
    slot, where = tables(pick_place, point_index.reshape(-1, 128))
    blocks = pick(pick_place, slot, where, orbitals, other)
    here = blocks[0] + to_y(blocks[1], 1) + to_y(blocks[3], 3) + to_y(blocks[2], 2)
    here, rows_here = lax.optimization_barrier((here, rows_here))
    around = [to_zh(here, 1), to_zh(here, 3), to_zh(here, 2)]
    pots = pack(place, potentials, other_pot)
    around, pots = lax.optimization_barrier((around, pots))
    here = here + around[0] + around[1] + around[2]
    beside = to_zl(here)
    pair = jnp.stack([here, beside])
    pieces = [pair] + [first_axis(pair, d) for d in (1, 2, 3)]
    rows = [rows_here, to_core(rows_here)]
    low, high = join(place, pieces)
    low_up, low_down = second_axis(low, 1), second_axis(low, 3)
    high_up, high_down = second_axis(high, 1), second_axis(high, 3)
    lows = [low, low_up, second_axis(low_up, 1), low_down]
    highs = [high, high_up, second_axis(high_down, 3), high_down]
    parts = apply(0, place, rows, pots, lows)
    (sent,) = apply(1, place, rows[1:], pots[1:], highs, parts[1], jnp.bfloat16)
    theirs = to_core(sent)
    (kept,) = apply(1, place, rows[:1], pots[:1], highs, parts[0])
    result = total(place, kept, theirs)
    return lax.all_to_all(result, "orb", split_axis=0, concat_axis=0, tiled=True).reshape(-1, 128)


def solution(mesh):
    return jax.shard_map(
        shards,
        mesh=mesh,
        in_specs=(P("grid", "orb"), P(("grid", "orb"), None), P()),
        out_specs=P("grid", "orb"),
        check_vma=False,
    )
```

```python
import functools

import jax
import jax.numpy as jnp
from jax import lax
from jax.experimental import pallas as pl
from jax.experimental.pallas import tpu as pltpu
from jax.sharding import PartitionSpec as P

NY, NZH, NC, NX, NZL = 4, 4, 2, 4, 2
AXES = ("grid", "orb")
BLOCK = 512
HALF = 256


def moves(target):
    pairs = []
    for y in range(NY):
        for zh in range(NZH):
            for c in range(NC):
                for x in range(NX):
                    for zl in range(NZL):
                        ty, tzh, tc, tx, tzl = target(y, zh, c, x, zl)
                        src = ((y * NZH + zh) * NC + c) * NX * NZL + x * NZL + zl
                        dst = ((ty % NY * NZH + tzh % NZH) * NC + tc % NC) * NX * NZL + tx % NX * NZL + tzl % NZL
                        pairs.append((src, dst))
    return pairs


def send(value, target):
    return lax.ppermute(value, AXES, moves(target))


def to_core(value):
    return send(value, lambda y, zh, c, x, zl: (y, zh, 1 - c, x, zl))


def to_y(value, d):
    return send(value, lambda y, zh, c, x, zl: (y ^ d, zh, c, x, zl))


def to_zh(value, d):
    return send(value, lambda y, zh, c, x, zl: (y, zh ^ d, c, x, zl))


def to_zl(value):
    return send(value, lambda y, zh, c, x, zl: (y, zh, c, x, 1 - zl))


def first_axis(value, d):
    return send(value, lambda y, zh, c, x, zl: (y ^ (d * c), zh, c, x ^ (d * (1 - c)), zl))


def second_axis(value, d):
    return send(value, lambda y, zh, c, x, zl: (y + d * (1 - c), zh, c, x + d * c, zl))


def table_kernel(place, index, slot_ref, where_ref):
    slab = place[0]
    idx = index[...]
    lines = idx.shape[0]
    owner = lax.shift_right_logical(idx, 12)
    in_mine = owner == slab
    in_other = owner == (slab ^ 1)
    flags = jnp.concatenate([in_mine.astype(jnp.float32), in_other.astype(jnp.float32)], axis=0)
    upper = (
        (lax.broadcasted_iota(jnp.int32, (128, 128), 0) <= lax.broadcasted_iota(jnp.int32, (128, 128), 1))
        .astype(jnp.float32)
        .astype(jnp.bfloat16)
    )
    counts = jnp.dot(flags.astype(jnp.bfloat16), upper, preferred_element_type=jnp.float32)
    totals = jnp.broadcast_to(counts[:, 127:128], (2 * lines, 128)).astype(jnp.bfloat16)
    to = lax.broadcasted_iota(jnp.int32, (2 * lines, 2 * lines), 0)
    of = lax.broadcasted_iota(jnp.int32, (2 * lines, 2 * lines), 1)
    earlier = ((of < to) & ((of < lines) == (to < lines))).astype(jnp.float32).astype(jnp.bfloat16)
    ranks = counts + jnp.dot(earlier, totals, preferred_element_type=jnp.float32) - 1.0
    slot = jnp.where(in_mine, ranks[:lines], jnp.where(in_other, ranks[lines:] + 256.0, -1.0)).astype(jnp.int32)
    slot_ref[...] = slot
    local = idx & 4095
    high = lax.shift_right_logical(local, 6).astype(jnp.float32)
    low = (local & 63).astype(jnp.float32)
    where = jnp.zeros((BLOCK, 8), jnp.float32)
    rows = lax.broadcasted_iota(jnp.int32, (BLOCK, BLOCK), 0)
    pick_row = lax.broadcasted_iota(jnp.int32, (8, BLOCK), 0)

    def line(value, b):
        return jnp.concatenate([value[i : i + 1, :] for i in range(4 * b, 4 * b + 4)], axis=1)

    for b in range(8):
        one_hot = (rows == line(slot, b)).astype(jnp.float32).astype(jnp.bfloat16)
        parts = jnp.where(pick_row == 0, line(high, b), jnp.where(pick_row == 1, line(low, b), 0.0))
        where = where + lax.dot_general(
            one_hot, parts.astype(jnp.bfloat16), (((1,), (1,)), ((), ())), preferred_element_type=jnp.float32
        )
    where_ref[...] = where


def tables(place, index):
    vmem = pl.BlockSpec(memory_space=pltpu.VMEM)
    return pl.pallas_call(
        table_kernel,
        out_shape=[jax.ShapeDtypeStruct(index.shape, jnp.int32), jax.ShapeDtypeStruct((BLOCK, 8), jnp.float32)],
        in_specs=[pl.BlockSpec(memory_space=pltpu.SMEM), vmem],
        out_specs=[vmem] * 2,
        compiler_params=pltpu.CompilerParams(vmem_limit_bytes=16 * 1024 * 1024),
        cost_estimate=pl.CostEstimate(flops=2_000_000_000, bytes_accessed=2_000_000, transcendentals=0),
        name="tables",
    )(place, index)


def pick_kernel(place, slot_ref, where_ref, mine, other_hbm, *refs):
    outs, other, other_sem = refs[:4], refs[4], refs[5]
    other_copy = pltpu.make_async_copy(other_hbm, other, other_sem)
    other_copy.start()
    half, y = place[1], place[2]
    where = where_ref[...]
    line = (where[:, 0:1] * 64.0 + where[:, 1:2]).astype(jnp.int32)
    picked = []
    wide = 1024
    lane = lax.broadcasted_iota(jnp.int32, (256, wide), 1)
    for s, block in enumerate((mine, other)):
        if s == 1:
            other_copy.wait()
        want = line[s * 256 : (s + 1) * 256, :]
        total = jnp.zeros((256, 128), jnp.float32)
        for k in range(4096 // wide):
            one_hot = (want - k * wide == lane).astype(jnp.float32).astype(jnp.bfloat16)
            total = total + jnp.dot(one_hot, block[k * wide : (k + 1) * wide, :], preferred_element_type=jnp.float32)
        picked.append(total)
    turned = jnp.concatenate(picked, axis=0).T.astype(jnp.bfloat16)
    rows = lax.broadcasted_iota(jnp.int32, (BLOCK, BLOCK), 0)
    for d in range(4):
        b = half * 4 + (y ^ d)
        four = slot_ref[pl.ds(b * 4, 4), :]
        row = jnp.concatenate([four[i : i + 1, :] for i in range(4)], axis=1)
        one_hot = (rows == row).astype(jnp.float32).astype(jnp.bfloat16)
        values = jnp.dot(turned, one_hot, preferred_element_type=jnp.float32).astype(jnp.bfloat16)
        outs[d][0] = values[:, :HALF]
        outs[d][1] = values[:, HALF:]


def pick(place, slot, where, mine, other):
    block = jax.ShapeDtypeStruct((2, 128, HALF), jnp.bfloat16)
    vmem = pl.BlockSpec(memory_space=pltpu.VMEM)
    return pl.pallas_call(
        pick_kernel,
        out_shape=[block] * 4,
        in_specs=[pl.BlockSpec(memory_space=pltpu.SMEM), vmem, vmem, vmem, pl.BlockSpec(memory_space=pl.ANY)],
        out_specs=[vmem] * 4,
        scratch_shapes=[pltpu.VMEM(other.shape, other.dtype), pltpu.SemaphoreType.DMA],
        compiler_params=pltpu.CompilerParams(vmem_limit_bytes=16 * 1024 * 1024),
        cost_estimate=pl.CostEstimate(flops=2_500_000_000, bytes_accessed=4_000_000, transcendentals=0),
        name="pick",
    )(place, slot, where, mine, other)


def join_kernel(place, *refs):
    pieces, messages = (refs[0], refs[3], refs[1], refs[2]), refs[4:6]
    core = place[2]
    for c in range(2):

        @pl.when(core == c)
        def _():
            for d in range(4):
                for dz in range(2):
                    for half in range(2):
                        value = pieces[d][dz, half]
                        if c == 0:
                            messages[half][d, dz] = value
                        else:
                            messages[d // 2][d % 2 * 2 + half, dz] = value


def join(place, pieces):
    vmem = pl.BlockSpec(memory_space=pltpu.VMEM)
    message = jax.ShapeDtypeStruct((4, 2, 128, HALF), jnp.bfloat16)
    return pl.pallas_call(
        join_kernel,
        out_shape=[message] * 2,
        in_specs=[pl.BlockSpec(memory_space=pltpu.SMEM)] + [vmem] * 4,
        out_specs=[vmem] * 2,
        compiler_params=pltpu.CompilerParams(vmem_limit_bytes=16 * 1024 * 1024),
        cost_estimate=pl.CostEstimate(flops=0, bytes_accessed=2_000_000, transcendentals=0),
        name="join",
    )(place, *pieces)


def pack_kernel(place, *refs):
    core = place[2]
    sources, outs, sem = refs[:2], refs[2:4], refs[4]
    copies = []
    for s in range(2):
        for b in range(8):
            lanes = pl.ds(pl.multiple_of((core * 8 + b) * HALF, HALF), HALF)
            copies.append(pltpu.make_async_copy(sources[s].at[:, lanes], outs[s].at[b], sem.at[s, b]))
    for copy in copies:
        copy.start()
    for copy in copies:
        copy.wait()


def pack(place, mine, theirs):
    anyspace = pl.BlockSpec(memory_space=pl.ANY)
    return pl.pallas_call(
        pack_kernel,
        out_shape=[jax.ShapeDtypeStruct((8, mine.shape[0], HALF), jnp.bfloat16)] * 2,
        in_specs=[pl.BlockSpec(memory_space=pltpu.SMEM), anyspace, anyspace],
        out_specs=[pl.BlockSpec(memory_space=pltpu.VMEM)] * 2,
        scratch_shapes=[pltpu.SemaphoreType.DMA((2, 8))],
        compiler_params=pltpu.CompilerParams(vmem_limit_bytes=16 * 1024 * 1024),
        cost_estimate=pl.CostEstimate(flops=0, bytes_accessed=8_000_000, transcendentals=0),
        name="pack",
    )(place, mine, theirs)


def low_block(core, y, e):
    return jnp.where(core == 0, ((y - e) & 3) * 2, (y ^ (e // 2)) * 2 + e % 2)


def high_block(core, y, e):
    return jnp.where(core == 0, ((y - e) & 3) * 2 + 1, (y ^ (2 + e // 2)) * 2 + e % 2)


def flat(message):
    return message[...].reshape(1024, HALF)


def square(message, k):
    return message[k].reshape(HALF, HALF)


def weigh(pots, block, density):
    each = density.shape[0] // len(pots)
    parts = [
        pot[block].astype(jnp.float32) * density[s * each : (s + 1) * each] for s, pot in enumerate(pots)
    ]
    return jnp.concatenate(parts, axis=0).astype(jnp.bfloat16)


def times(left, right):
    return jnp.dot(left, right, preferred_element_type=jnp.float32)


def spread(weighted, parts):
    return lax.dot_general(
        weighted, jnp.concatenate(parts, axis=1), (((1,), (1,)), ((), ())), preferred_element_type=jnp.float32
    )


def column_lanes(n):
    return slice(n * HALF, (n + 1) * HALF)


def whole_chunks(rows, pots, chunks, scratch):
    for k, (message, block) in enumerate(chunks):
        scratch[:, column_lanes(k)] = weigh(pots, block, times(rows[...], flat(message)))
    for n in range(4):
        yield n, spread(scratch[:, : len(chunks) * HALF], [square(message, n) for message, _ in chunks])


def early_kernel(
    place, mine, theirs, pot_mine, pot_theirs, low0, low1, high0, high3, rows, partial, out, scratch
):
    x, y, core, zl = place[0], place[1], place[2], place[3]
    each = mine.shape[1]
    pots = (pot_mine, pot_theirs)
    for k in range(8):
        block = jnp.where(core == 0, x ^ (k // 2), (x - k // 2) & 3) * 2 + (zl ^ (k % 2))
        lanes = slice(k * 128, (k + 1) * 128)
        rows[:each, lanes] = mine[block]
        rows[each:, lanes] = theirs[block]

    @pl.when(core == 0)
    def _():
        chunks = [(low0, low_block(core, y, 0)), (low1, low_block(core, y, 1))]
        chunks += [(high0, high_block(core, y, 0)), (high3, high_block(core, y, 3))]
        for n, total in whole_chunks(rows, pots, chunks, scratch):
            out[:, column_lanes(n)] = total

    @pl.when(core == 1)
    def _():
        for k in range(4):
            first = jnp.concatenate([square(low0, k), square(low1, k)], axis=0)
            out[:, column_lanes(k)] = times(rows[:, : 2 * HALF], first)
        for k in range(4):
            partial[:, column_lanes(k)] = times(rows[:, column_lanes(0)], square(high0, k)) + times(
                rows[:, column_lanes(3)], square(high3, k)
            )


def middle_kernel(place, rows, pot_mine, pot_theirs, before, low0, low1, low2, low3, out, scratch):
    y, core = place[1], place[2]
    pots = (pot_mine, pot_theirs)
    lows = (low0, low1, low2, low3)

    @pl.when(core == 0)
    def _():
        chunks = [(low2, low_block(core, y, 2)), (low3, low_block(core, y, 3))]
        for n, total in whole_chunks(rows, pots, chunks, scratch):
            out[:, column_lanes(n)] = before[:, column_lanes(n)] + total

    @pl.when(core == 1)
    def _():
        for k in range(4):
            rest = jnp.concatenate([square(low2, k), square(low3, k)], axis=0)
            density = before[:, column_lanes(k)] + times(rows[:, 2 * HALF :], rest)
            scratch[:, column_lanes(k)] = weigh(pots, low_block(core, y, k), density)
        for n in range(4):
            out[:, column_lanes(n)] = spread(scratch[...], [square(lows[n], k) for k in range(4)])


def late_kernel(side, place, rows, pot, before, partial, high0, high1, high2, high3, out, scratch):
    y, core = place[1], place[2]
    each = out.shape[0]
    part = slice(side * each, (side + 1) * each)
    highs = (high0, high1, high2, high3)

    @pl.when(core == 0)
    def _():
        chunks = [(high1, high_block(core, y, 1)), (high2, high_block(core, y, 2))]
        for n, total in whole_chunks(rows.at[part], (pot,), chunks, scratch):
            out[:, column_lanes(n)] = (before[part, column_lanes(n)] + total).astype(out.dtype)

    @pl.when(core == 1)
    def _():
        for k in range(4):
            rest = jnp.concatenate([square(high1, k), square(high2, k)], axis=0)
            density = partial[part, column_lanes(k)] + times(rows[part, HALF : 3 * HALF], rest)
            scratch[:, column_lanes(k)] = weigh((pot,), high_block(core, y, k), density)
        for n in range(4):
            total = spread(scratch[...], [square(highs[n], k) for k in range(4)])
            out[:, column_lanes(n)] = (before[part, column_lanes(n)] + total).astype(out.dtype)


def call(kernel, name, outs, work, *operands, aliases=None):
    vmem = pl.BlockSpec(memory_space=pltpu.VMEM)
    lines = outs[-1].shape[0]
    return pl.pallas_call(
        kernel,
        out_shape=outs,
        in_specs=[pl.BlockSpec(memory_space=pltpu.SMEM)] + [vmem] * (len(operands) - 1),
        out_specs=[vmem] * len(outs),
        scratch_shapes=[pltpu.VMEM((lines, 1024), jnp.bfloat16)],
        input_output_aliases=aliases or {},
        compiler_params=pltpu.CompilerParams(vmem_limit_bytes=16 * 1024 * 1024),
        cost_estimate=pl.CostEstimate(
            flops=work * lines * 1024 * 1024, bytes_accessed=4 * 1024 * 1024, transcendentals=0
        ),
        name=name,
    )(*operands)


def total_kernel(place, mine, theirs, out):
    x, core, zl = place[0], place[2], place[3]
    for k in range(8):
        first, second = x ^ (k // 2), (x - k // 2) & 3
        here = jnp.where(core == 0, first, second) * 256 + (zl ^ (k % 2)) * 128
        there = jnp.where(core == 0, second, first) * 256 + (zl ^ (k % 2)) * 128
        value = mine[:, pl.ds(pl.multiple_of(here, 128), 128)]
        value = value + theirs[:, pl.ds(pl.multiple_of(there, 128), 128)].astype(jnp.float32)
        out[k] = (-value).astype(jnp.bfloat16)


def total(place, mine, theirs):
    vmem = pl.BlockSpec(memory_space=pltpu.VMEM)
    return pl.pallas_call(
        total_kernel,
        out_shape=jax.ShapeDtypeStruct((8, mine.shape[0], 128), jnp.bfloat16),
        in_specs=[pl.BlockSpec(memory_space=pltpu.SMEM), vmem, vmem],
        out_specs=vmem,
        compiler_params=pltpu.CompilerParams(vmem_limit_bytes=16 * 1024 * 1024),
        name="total",
    )(place, mine, theirs)


def shards(orbitals, potentials, point_index):
    grid, orb = lax.axis_index("grid"), lax.axis_index("orb")
    c = lax.rem(grid, NC)
    y = lax.div(grid, NZH * NC)
    x, zl = lax.div(orb, NZL), lax.rem(orb, NZL)
    pick_place = jnp.stack([grid, c, y]).astype(jnp.int32)
    place = jnp.stack([x, y, c, zl]).astype(jnp.int32)

    other = to_core(orbitals)
    other_pot = to_core(potentials)
    rows_here = lax.all_to_all(orbitals.reshape(8, -1, 128), "orb", split_axis=0, concat_axis=0, tiled=True)
    slot, where = tables(pick_place, point_index.reshape(-1, 128))
    blocks = pick(pick_place, slot, where, orbitals, other)
    here = to_y(blocks[2], 2) + to_y(blocks[1], 1) + to_y(blocks[3], 3) + blocks[0]
    here, rows_here = lax.optimization_barrier((here, rows_here))
    around = [to_zh(here, 2), to_zh(here, 1), to_zh(here, 3)]
    pots = pack(place, potentials, other_pot)
    around, pots = lax.optimization_barrier((around, pots))
    here = here + around[0] + around[1] + around[2]
    beside = to_zl(here)
    pair = jnp.stack([here, beside])
    pair, rows_here = lax.optimization_barrier((pair, rows_here))
    rows = [rows_here, to_core(rows_here)]
    pieces = [pair] + [first_axis(pair, d) for d in (2, 3, 1)]
    low, high = join(place, pieces)
    low_up, low_down = second_axis(low, 1), second_axis(low, 3)
    high_up, high_down = second_axis(high, 1), second_axis(high, 3)
    lows = [low, low_up, second_axis(low_up, 1), low_down]
    highs = [high, high_up, second_axis(high_down, 3), high_down]
    each = potentials.shape[0]
    sums = jax.ShapeDtypeStruct((2 * each, 1024), jnp.float32)
    lines = jax.ShapeDtypeStruct((2 * each, 1024), jnp.bfloat16)
    low0, low1, low2, low3 = lows
    high0, high1, high2, high3 = highs
    lined, partial, early = call(
        early_kernel, "early", [lines, sums, sums], 3, place, *rows, *pots, low0, low1, high0, high3
    )
    (acc,) = call(
        middle_kernel, "middle", [sums], 3, place, lined, *pots, early, low0, low1, low2, low3, aliases={4: 0}
    )
    halves = []
    for side, dtype in ((1, jnp.bfloat16), (0, jnp.float32)):
        out = jax.ShapeDtypeStruct((each, 1024), dtype)
        kernel = functools.partial(late_kernel, side)
        halves += call(kernel, "late", [out], 3, place, lined, pots[side], acc, partial, *highs)
    sent, kept = halves
    theirs = to_core(sent)
    result = total(place, kept, theirs)
    return lax.all_to_all(result, "orb", split_axis=0, concat_axis=0, tiled=True).reshape(-1, 128)


def solution(mesh):
    return jax.shard_map(
        shards,
        mesh=mesh,
        in_specs=(P("grid", "orb"), P(("grid", "orb"), None), P()),
        out_specs=P("grid", "orb"),
        check_vma=False,
    )
```

```python
import functools

import jax
import jax.numpy as jnp
from jax import lax
from jax.experimental import pallas as pl
from jax.experimental.pallas import tpu as pltpu
from jax.sharding import PartitionSpec as P

NY, NZH, NC, NX, NZL = 4, 4, 2, 4, 2
AXES = ("grid", "orb")
BLOCK = 512
HALF = 256
ORDER = ((2, 1), (0, 1), (2, 0), (3, 1), (1, 1), (3, 0), (1, 0), (0, 0))


def moves(target):
    pairs = []
    for y in range(NY):
        for zh in range(NZH):
            for c in range(NC):
                for x in range(NX):
                    for zl in range(NZL):
                        ty, tzh, tc, tx, tzl = target(y, zh, c, x, zl)
                        src = ((y * NZH + zh) * NC + c) * NX * NZL + x * NZL + zl
                        dst = ((ty % NY * NZH + tzh % NZH) * NC + tc % NC) * NX * NZL + tx % NX * NZL + tzl % NZL
                        pairs.append((src, dst))
    return pairs


def send(value, target):
    return lax.ppermute(value, AXES, moves(target))


def to_core(value):
    return send(value, lambda y, zh, c, x, zl: (y, zh, 1 - c, x, zl))


def to_y(value, d):
    return send(value, lambda y, zh, c, x, zl: (y ^ d, zh, c, x, zl))


def to_zh(value, d):
    return send(value, lambda y, zh, c, x, zl: (y, zh ^ d, c, x, zl))


def to_zl(value):
    return send(value, lambda y, zh, c, x, zl: (y, zh, c, x, 1 - zl))


def first_axis(value, d):
    return send(value, lambda y, zh, c, x, zl: (y ^ (d * c), zh, c, x ^ (d * (1 - c)), zl))


def to_owner(value, d, dz):
    return send(value, lambda y, zh, c, x, zl: (y, zh, c, x ^ d, zl ^ dz))


def second_axis(value, d):
    return send(value, lambda y, zh, c, x, zl: (y + d * (1 - c), zh, c, x + d * c, zl))


def one_hot(places, wanted):
    one, zero = jnp.ones((), jnp.bfloat16), jnp.zeros((), jnp.bfloat16)
    return jnp.where(places == wanted.astype(jnp.int16), one, zero)


def table_kernel(place, index, slot_ref, where_ref):
    slab = place[0]
    idx = index[...]
    lines = idx.shape[0]
    owner = lax.shift_right_logical(idx, 12)
    in_mine = owner == slab
    in_other = owner == (slab ^ 1)
    flags = jnp.concatenate([in_mine.astype(jnp.float32), in_other.astype(jnp.float32)], axis=0)
    upper = (
        (lax.broadcasted_iota(jnp.int32, (128, 128), 0) <= lax.broadcasted_iota(jnp.int32, (128, 128), 1))
        .astype(jnp.float32)
        .astype(jnp.bfloat16)
    )
    counts = jnp.dot(flags.astype(jnp.bfloat16), upper, preferred_element_type=jnp.float32)
    totals = jnp.broadcast_to(counts[:, 127:128], (2 * lines, 128)).astype(jnp.bfloat16)
    to = lax.broadcasted_iota(jnp.int32, (2 * lines, 2 * lines), 0)
    of = lax.broadcasted_iota(jnp.int32, (2 * lines, 2 * lines), 1)
    earlier = ((of < to) & ((of < lines) == (to < lines))).astype(jnp.float32).astype(jnp.bfloat16)
    ranks = counts + jnp.dot(earlier, totals, preferred_element_type=jnp.float32) - 1.0
    slot = jnp.where(in_mine, ranks[:lines], jnp.where(in_other, ranks[lines:] + 256.0, -1.0)).astype(jnp.int32)
    slot_ref[...] = slot
    local = idx & 4095
    high = lax.shift_right_logical(local, 6).astype(jnp.float32)
    low = (local & 63).astype(jnp.float32)
    where = jnp.zeros((BLOCK, 8), jnp.float32)
    rows = lax.broadcasted_iota(jnp.int32, (BLOCK, BLOCK), 0).astype(jnp.int16)
    pick_row = lax.broadcasted_iota(jnp.int32, (8, BLOCK), 0)

    def line(value, b):
        return jnp.concatenate([value[i : i + 1, :] for i in range(4 * b, 4 * b + 4)], axis=1)

    for b in range(8):
        parts = jnp.where(pick_row == 0, line(high, b), jnp.where(pick_row == 1, line(low, b), 0.0))
        where = where + lax.dot_general(
            one_hot(rows, line(slot, b)), parts.astype(jnp.bfloat16), (((1,), (1,)), ((), ())), preferred_element_type=jnp.float32
        )
    where_ref[...] = where


def tables(place, index):
    vmem = pl.BlockSpec(memory_space=pltpu.VMEM)
    return pl.pallas_call(
        table_kernel,
        out_shape=[jax.ShapeDtypeStruct(index.shape, jnp.int32), jax.ShapeDtypeStruct((BLOCK, 8), jnp.float32)],
        in_specs=[pl.BlockSpec(memory_space=pltpu.SMEM), vmem],
        out_specs=[vmem] * 2,
        compiler_params=pltpu.CompilerParams(vmem_limit_bytes=16 * 1024 * 1024),
        cost_estimate=pl.CostEstimate(flops=2_000_000_000, bytes_accessed=2_000_000, transcendentals=0),
        name="tables",
    )(place, index)


def pick_kernel(place, slot_ref, where_ref, mine, other_hbm, *refs):
    outs, other, other_sem = refs[:4], refs[4], refs[5]
    other_copy = pltpu.make_async_copy(other_hbm, other, other_sem)
    other_copy.start()
    half, y = place[1], place[2]
    where = where_ref[...]
    line = (where[:, 0:1] * 64.0 + where[:, 1:2]).astype(jnp.int32)
    picked = []
    wide = 1024
    lane = lax.broadcasted_iota(jnp.int32, (256, wide), 1).astype(jnp.int16)
    for s, block in enumerate((mine, other)):
        if s == 1:
            other_copy.wait()
        want = line[s * 256 : (s + 1) * 256, :]
        total = jnp.zeros((256, 128), jnp.float32)
        for k in range(4096 // wide):
            chosen = one_hot(lane, want - k * wide)
            total = total + jnp.dot(chosen, block[k * wide : (k + 1) * wide, :], preferred_element_type=jnp.float32)
        picked.append(total)
    turned = jnp.concatenate(picked, axis=0).T.astype(jnp.bfloat16)
    rows = lax.broadcasted_iota(jnp.int32, (BLOCK, BLOCK), 0).astype(jnp.int16)
    for d in range(4):
        b = half * 4 + (y ^ d)
        four = slot_ref[pl.ds(b * 4, 4), :]
        row = jnp.concatenate([four[i : i + 1, :] for i in range(4)], axis=1)
        values = jnp.dot(turned, one_hot(rows, row), preferred_element_type=jnp.float32).astype(jnp.bfloat16)
        outs[d][0] = values[:, :HALF]
        outs[d][1] = values[:, HALF:]


def pick(place, slot, where, mine, other):
    block = jax.ShapeDtypeStruct((2, 128, HALF), jnp.bfloat16)
    vmem = pl.BlockSpec(memory_space=pltpu.VMEM)
    return pl.pallas_call(
        pick_kernel,
        out_shape=[block] * 4,
        in_specs=[pl.BlockSpec(memory_space=pltpu.SMEM), vmem, vmem, vmem, pl.BlockSpec(memory_space=pl.ANY)],
        out_specs=[vmem] * 4,
        scratch_shapes=[pltpu.VMEM(other.shape, other.dtype), pltpu.SemaphoreType.DMA],
        compiler_params=pltpu.CompilerParams(vmem_limit_bytes=16 * 1024 * 1024),
        cost_estimate=pl.CostEstimate(flops=2_500_000_000, bytes_accessed=4_000_000, transcendentals=0),
        name="pick",
    )(place, slot, where, mine, other)


def join_kernel(place, *refs):
    pieces, messages = (refs[0], refs[3], refs[1], refs[2]), refs[4:6]
    core = place[2]
    for c in range(2):

        @pl.when(core == c)
        def _():
            for d in range(4):
                for dz in range(2):
                    for half in range(2):
                        value = pieces[d][dz, half]
                        if c == 0:
                            messages[half][d, dz] = value
                        else:
                            messages[d // 2][d % 2 * 2 + half, dz] = value


def join(place, pieces):
    vmem = pl.BlockSpec(memory_space=pltpu.VMEM)
    message = jax.ShapeDtypeStruct((4, 2, 128, HALF), jnp.bfloat16)
    return pl.pallas_call(
        join_kernel,
        out_shape=[message] * 2,
        in_specs=[pl.BlockSpec(memory_space=pltpu.SMEM)] + [vmem] * 4,
        out_specs=[vmem] * 2,
        compiler_params=pltpu.CompilerParams(vmem_limit_bytes=16 * 1024 * 1024),
        cost_estimate=pl.CostEstimate(flops=0, bytes_accessed=2_000_000, transcendentals=0),
        name="join",
    )(place, *pieces)


def pack_kernel(place, *refs):
    core = place[2]
    sources, outs, sem = refs[:2], refs[2:4], refs[4]
    copies = []
    for s in range(2):
        for b in range(8):
            lanes = pl.ds(pl.multiple_of((core * 8 + b) * HALF, HALF), HALF)
            copies.append(pltpu.make_async_copy(sources[s].at[:, lanes], outs[s].at[b], sem.at[s, b]))
    for copy in copies:
        copy.start()
    for copy in copies:
        copy.wait()


def pack(place, mine, theirs):
    anyspace = pl.BlockSpec(memory_space=pl.ANY)
    return pl.pallas_call(
        pack_kernel,
        out_shape=[jax.ShapeDtypeStruct((8, mine.shape[0], HALF), jnp.bfloat16)] * 2,
        in_specs=[pl.BlockSpec(memory_space=pltpu.SMEM), anyspace, anyspace],
        out_specs=[pl.BlockSpec(memory_space=pltpu.VMEM)] * 2,
        scratch_shapes=[pltpu.SemaphoreType.DMA((2, 8))],
        compiler_params=pltpu.CompilerParams(vmem_limit_bytes=16 * 1024 * 1024),
        cost_estimate=pl.CostEstimate(flops=0, bytes_accessed=8_000_000, transcendentals=0),
        name="pack",
    )(place, mine, theirs)


def low_block(core, y, e):
    return jnp.where(core == 0, ((y - e) & 3) * 2, (y ^ (e // 2)) * 2 + e % 2)


def high_block(core, y, e):
    return jnp.where(core == 0, ((y - e) & 3) * 2 + 1, (y ^ (2 + e // 2)) * 2 + e % 2)


def flat(message):
    return message[...].reshape(1024, HALF)


def square(message, k):
    return message[k].reshape(HALF, HALF)


def weigh(pots, block, density):
    each = density.shape[0] // len(pots)
    parts = [
        pot[block].astype(jnp.float32) * density[s * each : (s + 1) * each] for s, pot in enumerate(pots)
    ]
    return jnp.concatenate(parts, axis=0).astype(jnp.bfloat16)


def times(left, right):
    return jnp.dot(left, right, preferred_element_type=jnp.float32)


def spread(weighted, parts):
    return lax.dot_general(
        weighted, jnp.concatenate(parts, axis=1), (((1,), (1,)), ((), ())), preferred_element_type=jnp.float32
    )


def column_lanes(n):
    return slice(n * HALF, (n + 1) * HALF)


def whole_chunks(rows, pots, chunks, scratch):
    for k, (message, block) in enumerate(chunks):
        scratch[:, column_lanes(k)] = weigh(pots, block, times(rows[...], flat(message)))
    for n in range(4):
        yield n, spread(scratch[:, : len(chunks) * HALF], [square(message, n) for message, _ in chunks])


def early_kernel(
    place, mine, theirs, pot_mine, pot_theirs, low0, low1, high0, high3, rows, partial, out, scratch
):
    x, y, core, zl = place[0], place[1], place[2], place[3]
    each = mine.shape[1]
    pots = (pot_mine, pot_theirs)
    for k in range(8):
        block = jnp.where(core == 0, x ^ (k // 2), (x - k // 2) & 3) * 2 + (zl ^ (k % 2))
        lanes = slice(k * 128, (k + 1) * 128)
        rows[:each, lanes] = mine[block]
        rows[each:, lanes] = theirs[block]

    @pl.when(core == 0)
    def _():
        chunks = [(low0, low_block(core, y, 0)), (low1, low_block(core, y, 1))]
        chunks += [(high0, high_block(core, y, 0)), (high3, high_block(core, y, 3))]
        for n, total in whole_chunks(rows, pots, chunks, scratch):
            out[:, column_lanes(n)] = total

    @pl.when(core == 1)
    def _():
        for k in range(4):
            first = jnp.concatenate([square(low0, k), square(low1, k)], axis=0)
            out[:, column_lanes(k)] = times(rows[:, : 2 * HALF], first)
            partial[:, column_lanes(k)] = times(rows[:, column_lanes(0)], square(high0, k)) + times(
                rows[:, column_lanes(3)], square(high3, k)
            )


def middle_kernel(place, rows, pot_mine, pot_theirs, low_before, high_before, low3, high1, partial, out, scratch):
    y, core = place[1], place[2]

    @pl.when(core == 0)
    def _():
        chunks = [(low3, low_block(core, y, 3)), (high1, high_block(core, y, 1))]
        for n, total in whole_chunks(rows, (pot_mine, pot_theirs), chunks, scratch):
            out[:, column_lanes(n)] = low_before[:, column_lanes(n)] + total

    @pl.when(core == 1)
    def _():
        for k in range(4):
            lanes = column_lanes(k)
            out[:, lanes] = low_before[:, lanes] + times(rows[:, column_lanes(3)], square(low3, k))
            partial[:, lanes] = high_before[:, lanes] + times(rows[:, column_lanes(1)], square(high1, k))


def late_kernel(side, place, rows, pot, before, partial, *refs):
    lows, highs, (out, scratch) = refs[:4], refs[4:8], refs[8:]
    y, core = place[1], place[2]
    each = out.shape[0]
    part = slice(side * each, (side + 1) * each)

    @pl.when(core == 0)
    def _():
        chunks = [(lows[2], low_block(core, y, 2)), (highs[2], high_block(core, y, 2))]
        for n, total in whole_chunks(rows.at[part], (pot,), chunks, scratch):
            out[:, column_lanes(n)] = (before[part, column_lanes(n)] + total).astype(out.dtype)

    @pl.when(core == 1)
    def _():
        for i, (known, messages, where) in enumerate(((before, lows, low_block), (partial, highs, high_block))):
            for k in range(4):
                density = known[part, column_lanes(k)] + times(rows[part, column_lanes(2)], square(messages[2], k))
                scratch[:, column_lanes(4 * i + k)] = weigh((pot,), where(core, y, k), density)
        for n in range(4):
            parts = [square(lows[n], k) for k in range(4)] + [square(highs[n], k) for k in range(4)]
            out[:, column_lanes(n)] = spread(scratch[...], parts).astype(out.dtype)


def call(kernel, name, outs, work, *operands, aliases=None):
    vmem = pl.BlockSpec(memory_space=pltpu.VMEM)
    lines = outs[-1].shape[0]
    return pl.pallas_call(
        kernel,
        out_shape=outs,
        in_specs=[pl.BlockSpec(memory_space=pltpu.SMEM)] + [vmem] * (len(operands) - 1),
        out_specs=[vmem] * len(outs),
        scratch_shapes=[pltpu.VMEM((lines, 2048), jnp.bfloat16)],
        input_output_aliases=aliases or {},
        compiler_params=pltpu.CompilerParams(vmem_limit_bytes=16 * 1024 * 1024),
        cost_estimate=pl.CostEstimate(
            flops=work * lines * 1024 * 1024, bytes_accessed=4 * 1024 * 1024, transcendentals=0
        ),
        name=name,
    )(*operands)


def total_kernel(place, mine, theirs, *outs):
    x, core = place[0], place[2]
    for d in range(4):
        other = (x - (x ^ d)) & 3
        here, there = jnp.where(core == 0, d, other), jnp.where(core == 0, other, d)
        for dz in range(2):
            value = mine[:, pl.ds(pl.multiple_of(here * 256 + dz * 128, 128), 128)]
            value = value + theirs[:, pl.ds(pl.multiple_of(there * 256 + dz * 128, 128), 128)].astype(jnp.float32)
            outs[2 * d + dz][...] = (-value).astype(jnp.bfloat16)


def total(place, mine, theirs):
    vmem = pl.BlockSpec(memory_space=pltpu.VMEM)
    return pl.pallas_call(
        total_kernel,
        out_shape=[jax.ShapeDtypeStruct((mine.shape[0], 128), jnp.bfloat16)] * 8,
        in_specs=[pl.BlockSpec(memory_space=pltpu.SMEM), vmem, vmem],
        out_specs=[vmem] * 8,
        compiler_params=pltpu.CompilerParams(vmem_limit_bytes=16 * 1024 * 1024),
        name="total",
    )(place, mine, theirs)


def put_kernel(place, *refs):
    blocks, out, sem = refs[:8], refs[8], refs[9]
    x, zl = place[0], place[3]
    copies = []
    for i, (d, dz) in enumerate(ORDER):
        run = (x ^ d) * 2 + (zl ^ dz)
        copies.append(pltpu.make_async_copy(blocks[i], out.at[run], sem.at[i]))
    for copy in copies:
        copy.start()
    for copy in copies:
        copy.wait()


def put(place, blocks):
    vmem = pl.BlockSpec(memory_space=pltpu.VMEM)
    return pl.pallas_call(
        put_kernel,
        out_shape=jax.ShapeDtypeStruct((8,) + blocks[0].shape, jnp.bfloat16),
        in_specs=[pl.BlockSpec(memory_space=pltpu.SMEM)] + [vmem] * 8,
        out_specs=pl.BlockSpec(memory_space=pl.ANY),
        scratch_shapes=[pltpu.SemaphoreType.DMA((8,))],
        compiler_params=pltpu.CompilerParams(vmem_limit_bytes=16 * 1024 * 1024),
        name="put",
    )(place, *blocks)


def shards(orbitals, potentials, point_index):
    grid, orb = lax.axis_index("grid"), lax.axis_index("orb")
    c = lax.rem(grid, NC)
    y = lax.div(grid, NZH * NC)
    x, zl = lax.div(orb, NZL), lax.rem(orb, NZL)
    pick_place = jnp.stack([grid, c, y]).astype(jnp.int32)
    place = jnp.stack([x, y, c, zl]).astype(jnp.int32)

    other = to_core(orbitals)
    other_pot = to_core(potentials)
    rows_here = lax.all_to_all(orbitals.reshape(8, -1, 128), "orb", split_axis=0, concat_axis=0, tiled=True)
    slot, where = tables(pick_place, point_index.reshape(-1, 128))
    blocks = pick(pick_place, slot, where, orbitals, other)
    here = to_y(blocks[2], 2) + to_y(blocks[3], 3) + to_y(blocks[1], 1) + blocks[0]
    here, rows_here = lax.optimization_barrier((here, rows_here))
    around = [to_zh(here, 2), to_zh(here, 3), to_zh(here, 1)]
    pots = pack(place, potentials, other_pot)
    around, pots = lax.optimization_barrier((around, pots))
    here = here + around[0] + around[1] + around[2]
    beside = to_zl(here)
    pair = jnp.stack([here, beside])
    pair, rows_here = lax.optimization_barrier((pair, rows_here))
    rows = [rows_here, to_core(rows_here)]
    pieces = [pair] + [first_axis(pair, d) for d in (2, 3, 1)]
    low, high = join(place, pieces)
    low_up, low_down = second_axis(low, 1), second_axis(low, 3)
    high_up, high_down = second_axis(high, 1), second_axis(high, 3)
    lows = [low, low_up, second_axis(low_up, 1), low_down]
    highs = [high, high_up, second_axis(high_down, 3), high_down]
    each = potentials.shape[0]
    sums = jax.ShapeDtypeStruct((2 * each, 1024), jnp.float32)
    lines = jax.ShapeDtypeStruct((2 * each, 1024), jnp.bfloat16)
    low0, low1, low2, low3 = lows
    high0, high1, high2, high3 = highs
    near = [low0, low1, high0, high3]
    lined, partial, early = call(early_kernel, "early", [lines, sums, sums], 3, place, *rows, *pots, *near)
    partial, early = call(
        middle_kernel, "middle", [sums, sums], 2, place, lined, *pots, early, partial, low3, high1, aliases={5: 0, 4: 1}
    )
    halves = []
    for side, dtype in ((1, jnp.bfloat16), (0, jnp.float32)):
        out = jax.ShapeDtypeStruct((each, 1024), dtype)
        kernel = functools.partial(late_kernel, side)
        halves += call(kernel, "late", [out], 3, place, lined, pots[side], early, partial, *lows, *highs)
    sent, kept = halves
    theirs = to_core(sent)
    blocks = total(place, kept, theirs)
    arrived = [to_owner(blocks[2 * d + dz], d, dz) for d, dz in ORDER[:-1]] + [blocks[0]]
    return put(place, arrived).reshape(-1, 128)


def solution(mesh):
    return jax.shard_map(
        shards,
        mesh=mesh,
        in_specs=(P("grid", "orb"), P(("grid", "orb"), None), P()),
        out_specs=P("grid", "orb"),
        check_vma=False,
    )
```

```python
import functools

import jax
import jax.numpy as jnp
from jax import lax
from jax.experimental import pallas as pl
from jax.experimental.pallas import tpu as pltpu
from jax.sharding import PartitionSpec as P

NY, NZH, NC, NX, NZL = 4, 4, 2, 4, 2
AXES = ("grid", "orb")
BLOCK = 512
HALF = 256
ORDER = ((2, 1), (0, 1), (2, 0), (3, 1), (1, 1), (3, 0), (1, 0), (0, 0))


def moves(target):
    pairs = []
    for y in range(NY):
        for zh in range(NZH):
            for c in range(NC):
                for x in range(NX):
                    for zl in range(NZL):
                        ty, tzh, tc, tx, tzl = target(y, zh, c, x, zl)
                        src = ((y * NZH + zh) * NC + c) * NX * NZL + x * NZL + zl
                        dst = ((ty % NY * NZH + tzh % NZH) * NC + tc % NC) * NX * NZL + tx % NX * NZL + tzl % NZL
                        pairs.append((src, dst))
    return pairs


def send(value, target):
    return lax.ppermute(value, AXES, moves(target))


def to_core(value):
    return send(value, lambda y, zh, c, x, zl: (y, zh, 1 - c, x, zl))


def to_y(value, d):
    return send(value, lambda y, zh, c, x, zl: (y ^ d, zh, c, x, zl))


def to_zh(value, d):
    return send(value, lambda y, zh, c, x, zl: (y, zh ^ d, c, x, zl))


def to_zl(value):
    return send(value, lambda y, zh, c, x, zl: (y, zh, c, x, 1 - zl))


def first_axis(value, d):
    return send(value, lambda y, zh, c, x, zl: (y ^ (d * c), zh, c, x ^ (d * (1 - c)), zl))


def to_owner(value, d, dz):
    return send(value, lambda y, zh, c, x, zl: (y, zh, c, x ^ d, zl ^ dz))


def second_axis(value, d):
    return send(value, lambda y, zh, c, x, zl: (y + d * (1 - c), zh, c, x + d * c, zl))


def one_hot(places, wanted):
    one, zero = jnp.ones((), jnp.bfloat16), jnp.zeros((), jnp.bfloat16)
    return jnp.where(places == wanted.astype(jnp.int16), one, zero)


def table_kernel(place, index, slot_ref, where_ref):
    slab = place[0]
    idx = index[...]
    lines = idx.shape[0]
    owner = lax.shift_right_logical(idx, 12)
    in_mine = owner == slab
    in_other = owner == (slab ^ 1)
    flags = jnp.concatenate([in_mine.astype(jnp.float32), in_other.astype(jnp.float32)], axis=0)
    upper = (
        (lax.broadcasted_iota(jnp.int32, (128, 128), 0) <= lax.broadcasted_iota(jnp.int32, (128, 128), 1))
        .astype(jnp.float32)
        .astype(jnp.bfloat16)
    )
    counts = jnp.dot(flags.astype(jnp.bfloat16), upper, preferred_element_type=jnp.float32)
    totals = jnp.broadcast_to(counts[:, 127:128], (2 * lines, 128)).astype(jnp.bfloat16)
    to = lax.broadcasted_iota(jnp.int32, (2 * lines, 2 * lines), 0)
    of = lax.broadcasted_iota(jnp.int32, (2 * lines, 2 * lines), 1)
    earlier = ((of < to) & ((of < lines) == (to < lines))).astype(jnp.float32).astype(jnp.bfloat16)
    ranks = counts + jnp.dot(earlier, totals, preferred_element_type=jnp.float32) - 1.0
    slot = jnp.where(in_mine, ranks[:lines], jnp.where(in_other, ranks[lines:] + 256.0, -1.0)).astype(jnp.int32)
    slot_ref[...] = slot
    local = idx & 4095
    high = lax.shift_right_logical(local, 6).astype(jnp.float32)
    low = (local & 63).astype(jnp.float32)
    where = jnp.zeros((BLOCK, 8), jnp.float32)
    rows = lax.broadcasted_iota(jnp.int32, (BLOCK, BLOCK), 0).astype(jnp.int16)
    pick_row = lax.broadcasted_iota(jnp.int32, (8, BLOCK), 0)

    def line(value, b):
        return jnp.concatenate([value[i : i + 1, :] for i in range(4 * b, 4 * b + 4)], axis=1)

    for b in range(8):
        parts = jnp.where(pick_row == 0, line(high, b), jnp.where(pick_row == 1, line(low, b), 0.0))
        where = where + lax.dot_general(
            one_hot(rows, line(slot, b)), parts.astype(jnp.bfloat16), (((1,), (1,)), ((), ())), preferred_element_type=jnp.float32
        )
    where_ref[...] = where


def tables(place, index):
    vmem = pl.BlockSpec(memory_space=pltpu.VMEM)
    return pl.pallas_call(
        table_kernel,
        out_shape=[jax.ShapeDtypeStruct(index.shape, jnp.int32), jax.ShapeDtypeStruct((BLOCK, 8), jnp.float32)],
        in_specs=[pl.BlockSpec(memory_space=pltpu.SMEM), vmem],
        out_specs=[vmem] * 2,
        compiler_params=pltpu.CompilerParams(vmem_limit_bytes=16 * 1024 * 1024),
        cost_estimate=pl.CostEstimate(flops=2_000_000_000, bytes_accessed=2_000_000, transcendentals=0),
        name="tables",
    )(place, index)


def pick_kernel(place, slot_ref, where_ref, mine, other_hbm, *refs):
    outs, other, other_sem = refs[:4], refs[4], refs[5]
    other_copy = pltpu.make_async_copy(other_hbm, other, other_sem)
    other_copy.start()
    half, y = place[1], place[2]
    where = where_ref[...]
    line = (where[:, 0:1] * 64.0 + where[:, 1:2]).astype(jnp.int32)
    picked = []
    wide = 1024
    lane = lax.broadcasted_iota(jnp.int32, (256, wide), 1).astype(jnp.int16)
    for s, block in enumerate((mine, other)):
        if s == 1:
            other_copy.wait()
        want = line[s * 256 : (s + 1) * 256, :]
        total = jnp.zeros((256, 128), jnp.float32)
        for k in range(4096 // wide):
            chosen = one_hot(lane, want - k * wide)
            total = total + jnp.dot(chosen, block[k * wide : (k + 1) * wide, :], preferred_element_type=jnp.float32)
        picked.append(total)
    turned = jnp.concatenate(picked, axis=0).T.astype(jnp.bfloat16)
    rows = lax.broadcasted_iota(jnp.int32, (BLOCK, BLOCK), 0).astype(jnp.int16)
    for d in range(4):
        b = half * 4 + (y ^ d)
        four = slot_ref[pl.ds(b * 4, 4), :]
        row = jnp.concatenate([four[i : i + 1, :] for i in range(4)], axis=1)
        values = jnp.dot(turned, one_hot(rows, row), preferred_element_type=jnp.float32).astype(jnp.bfloat16)
        outs[d][0] = values[:, :HALF]
        outs[d][1] = values[:, HALF:]


def pick(place, slot, where, mine, other):
    block = jax.ShapeDtypeStruct((2, 128, HALF), jnp.bfloat16)
    vmem = pl.BlockSpec(memory_space=pltpu.VMEM)
    return pl.pallas_call(
        pick_kernel,
        out_shape=[block] * 4,
        in_specs=[pl.BlockSpec(memory_space=pltpu.SMEM), vmem, vmem, vmem, pl.BlockSpec(memory_space=pl.ANY)],
        out_specs=[vmem] * 4,
        scratch_shapes=[pltpu.VMEM(other.shape, other.dtype), pltpu.SemaphoreType.DMA],
        compiler_params=pltpu.CompilerParams(vmem_limit_bytes=16 * 1024 * 1024),
        cost_estimate=pl.CostEstimate(flops=2_500_000_000, bytes_accessed=4_000_000, transcendentals=0),
        name="pick",
    )(place, slot, where, mine, other)


def join_kernel(place, *refs):
    pieces, messages = (refs[0], refs[3], refs[1], refs[2]), refs[4:6]
    core = place[2]
    for c in range(2):

        @pl.when(core == c)
        def _():
            for d in range(4):
                for dz in range(2):
                    for half in range(2):
                        value = pieces[d][dz, half]
                        if c == 0:
                            messages[half][d, dz] = value
                        else:
                            messages[d // 2][d % 2 * 2 + half, dz] = value


def join(place, pieces):
    vmem = pl.BlockSpec(memory_space=pltpu.VMEM)
    message = jax.ShapeDtypeStruct((4, 2, 128, HALF), jnp.bfloat16)
    return pl.pallas_call(
        join_kernel,
        out_shape=[message] * 2,
        in_specs=[pl.BlockSpec(memory_space=pltpu.SMEM)] + [vmem] * 4,
        out_specs=[vmem] * 2,
        compiler_params=pltpu.CompilerParams(vmem_limit_bytes=16 * 1024 * 1024),
        cost_estimate=pl.CostEstimate(flops=0, bytes_accessed=2_000_000, transcendentals=0),
        name="join",
    )(place, *pieces)


def pack_kernel(place, *refs):
    core = place[2]
    sources, outs, sem = refs[:2], refs[2:4], refs[4]
    copies = []
    for s in range(2):
        for b in range(8):
            lanes = pl.ds(pl.multiple_of((core * 8 + b) * HALF, HALF), HALF)
            copies.append(pltpu.make_async_copy(sources[s].at[:, lanes], outs[s].at[b], sem.at[s, b]))
    for copy in copies:
        copy.start()
    for copy in copies:
        copy.wait()


def pack(place, mine, theirs):
    anyspace = pl.BlockSpec(memory_space=pl.ANY)
    return pl.pallas_call(
        pack_kernel,
        out_shape=[jax.ShapeDtypeStruct((8, mine.shape[0], HALF), jnp.bfloat16)] * 2,
        in_specs=[pl.BlockSpec(memory_space=pltpu.SMEM), anyspace, anyspace],
        out_specs=[pl.BlockSpec(memory_space=pltpu.VMEM)] * 2,
        scratch_shapes=[pltpu.SemaphoreType.DMA((2, 8))],
        compiler_params=pltpu.CompilerParams(vmem_limit_bytes=16 * 1024 * 1024),
        cost_estimate=pl.CostEstimate(flops=0, bytes_accessed=8_000_000, transcendentals=0),
        name="pack",
    )(place, mine, theirs)


def low_block(core, y, e):
    return jnp.where(core == 0, ((y - e) & 3) * 2, (y ^ (e // 2)) * 2 + e % 2)


def high_block(core, y, e):
    return jnp.where(core == 0, ((y - e) & 3) * 2 + 1, (y ^ (2 + e // 2)) * 2 + e % 2)


def flat(message):
    return message[...].reshape(1024, HALF)


def square(message, k):
    return message[k].reshape(HALF, HALF)


def weigh(pots, block, density):
    each = density.shape[0] // len(pots)
    parts = [
        pot[block].astype(jnp.float32) * density[s * each : (s + 1) * each] for s, pot in enumerate(pots)
    ]
    return jnp.concatenate(parts, axis=0).astype(jnp.bfloat16)


def times(left, right):
    return jnp.dot(left, right, preferred_element_type=jnp.float32)


def spread(weighted, parts):
    return lax.dot_general(
        weighted, jnp.concatenate(parts, axis=1), (((1,), (1,)), ((), ())), preferred_element_type=jnp.float32
    )


def column_lanes(n):
    return slice(n * HALF, (n + 1) * HALF)


def whole_chunks(rows, pots, chunks, scratch):
    for k, (message, block) in enumerate(chunks):
        scratch[:, column_lanes(k)] = weigh(pots, block, times(rows[...], flat(message)))
    for n in range(4):
        yield n, spread(scratch[:, : len(chunks) * HALF], [square(message, n) for message, _ in chunks])


def early_kernel(
    place, mine, theirs, pot_mine, pot_theirs, low0, low1, high0, high3, rows, partial, out, scratch
):
    x, y, core, zl = place[0], place[1], place[2], place[3]
    each = mine.shape[1]
    pots = (pot_mine, pot_theirs)
    for k in range(8):
        block = jnp.where(core == 0, x ^ (k // 2), (x - k // 2) & 3) * 2 + (zl ^ (k % 2))
        lanes = slice(k * 128, (k + 1) * 128)
        rows[:each, lanes] = mine[block]
        rows[each:, lanes] = theirs[block]

    @pl.when(core == 0)
    def _():
        chunks = [(low0, low_block(core, y, 0)), (low1, low_block(core, y, 1))]
        chunks += [(high0, high_block(core, y, 0)), (high3, high_block(core, y, 3))]
        for n, total in whole_chunks(rows, pots, chunks, scratch):
            out[:, column_lanes(n)] = total

    @pl.when(core == 1)
    def _():
        for k in range(4):
            first = jnp.concatenate([square(low0, k), square(low1, k)], axis=0)
            out[:, column_lanes(k)] = times(rows[:, : 2 * HALF], first)
            partial[:, column_lanes(k)] = times(rows[:, column_lanes(0)], square(high0, k)) + times(
                rows[:, column_lanes(3)], square(high3, k)
            )


def middle_kernel(place, rows, pot_mine, pot_theirs, low_before, high_before, low3, high1, partial, out, scratch):
    y, core = place[1], place[2]

    @pl.when(core == 0)
    def _():
        chunks = [(low3, low_block(core, y, 3)), (high1, high_block(core, y, 1))]
        for n, total in whole_chunks(rows, (pot_mine, pot_theirs), chunks, scratch):
            out[:, column_lanes(n)] = low_before[:, column_lanes(n)] + total

    @pl.when(core == 1)
    def _():
        for k in range(4):
            lanes = column_lanes(k)
            out[:, lanes] = low_before[:, lanes] + times(rows[:, column_lanes(3)], square(low3, k))
            partial[:, lanes] = high_before[:, lanes] + times(rows[:, column_lanes(1)], square(high1, k))


def late_kernel(side, place, rows, pot, before, partial, *refs):
    lows, highs, (out, scratch) = refs[:4], refs[4:8], refs[8:]
    y, core = place[1], place[2]
    each = out.shape[0]
    part = slice(side * each, (side + 1) * each)

    @pl.when(core == 0)
    def _():
        chunks = [(lows[2], low_block(core, y, 2)), (highs[2], high_block(core, y, 2))]
        for n, total in whole_chunks(rows.at[part], (pot,), chunks, scratch):
            out[:, column_lanes(n)] = (before[part, column_lanes(n)] + total).astype(out.dtype)

    @pl.when(core == 1)
    def _():
        for i, (known, messages, where) in enumerate(((before, lows, low_block), (partial, highs, high_block))):
            for k in range(4):
                density = known[part, column_lanes(k)] + times(rows[part, column_lanes(2)], square(messages[2], k))
                scratch[:, column_lanes(4 * i + k)] = weigh((pot,), where(core, y, k), density)
        for n in range(4):
            parts = [square(lows[n], k) for k in range(4)] + [square(highs[n], k) for k in range(4)]
            out[:, column_lanes(n)] = spread(scratch[...], parts).astype(out.dtype)


def call(kernel, name, outs, work, *operands, aliases=None):
    vmem = pl.BlockSpec(memory_space=pltpu.VMEM)
    lines = outs[-1].shape[0]
    return pl.pallas_call(
        kernel,
        out_shape=outs,
        in_specs=[pl.BlockSpec(memory_space=pltpu.SMEM)] + [vmem] * (len(operands) - 1),
        out_specs=[vmem] * len(outs),
        scratch_shapes=[pltpu.VMEM((lines, 2048), jnp.bfloat16)],
        input_output_aliases=aliases or {},
        compiler_params=pltpu.CompilerParams(vmem_limit_bytes=16 * 1024 * 1024),
        cost_estimate=pl.CostEstimate(
            flops=work * lines * 1024 * 1024, bytes_accessed=4 * 1024 * 1024, transcendentals=0
        ),
        name=name,
    )(*operands)


def total_kernel(place, mine, theirs, *outs):
    x, core = place[0], place[2]
    for d in range(4):
        other = (x - (x ^ d)) & 3
        here, there = jnp.where(core == 0, d, other), jnp.where(core == 0, other, d)
        for dz in range(2):
            value = mine[:, pl.ds(pl.multiple_of(here * 256 + dz * 128, 128), 128)]
            value = value + theirs[:, pl.ds(pl.multiple_of(there * 256 + dz * 128, 128), 128)].astype(jnp.float32)
            outs[2 * d + dz][...] = (-value).astype(jnp.bfloat16)


def total(place, mine, theirs):
    vmem = pl.BlockSpec(memory_space=pltpu.VMEM)
    return pl.pallas_call(
        total_kernel,
        out_shape=[jax.ShapeDtypeStruct((mine.shape[0], 128), jnp.bfloat16)] * 8,
        in_specs=[pl.BlockSpec(memory_space=pltpu.SMEM), vmem, vmem],
        out_specs=[vmem] * 8,
        compiler_params=pltpu.CompilerParams(vmem_limit_bytes=16 * 1024 * 1024),
        name="total",
    )(place, mine, theirs)


def put_kernel(order, place, *refs):
    blocks, out, sem = refs[: len(order)], refs[-2], refs[-1]
    x, zl = place[0], place[3]
    copies = []
    for i, (d, dz) in enumerate(order):
        run = (x ^ d) * 2 + (zl ^ dz)
        copies.append(pltpu.make_async_copy(blocks[i], out.at[run], sem.at[i]))
    for copy in copies:
        copy.start()
    for copy in copies:
        copy.wait()


def put(order, place, blocks, before=None):
    vmem = pl.BlockSpec(memory_space=pltpu.VMEM)
    anyspace = pl.BlockSpec(memory_space=pl.ANY)
    number = len(order)
    return pl.pallas_call(
        functools.partial(put_kernel, order),
        out_shape=jax.ShapeDtypeStruct((8,) + blocks[0].shape, jnp.bfloat16),
        in_specs=[pl.BlockSpec(memory_space=pltpu.SMEM)] + [vmem] * number + [anyspace] * (before is not None),
        out_specs=anyspace,
        scratch_shapes=[pltpu.SemaphoreType.DMA((number,))],
        input_output_aliases={} if before is None else {number + 1: 0},
        compiler_params=pltpu.CompilerParams(vmem_limit_bytes=16 * 1024 * 1024),
        cost_estimate=pl.CostEstimate(flops=0, bytes_accessed=number * 300_000, transcendentals=0),
        name="put",
    )(place, *blocks, *([] if before is None else [before]))


def shards(orbitals, potentials, point_index):
    grid, orb = lax.axis_index("grid"), lax.axis_index("orb")
    c = lax.rem(grid, NC)
    y = lax.div(grid, NZH * NC)
    x, zl = lax.div(orb, NZL), lax.rem(orb, NZL)
    pick_place = jnp.stack([grid, c, y]).astype(jnp.int32)
    place = jnp.stack([x, y, c, zl]).astype(jnp.int32)

    other = to_core(orbitals)
    other_pot = to_core(potentials)
    rows_here = lax.all_to_all(orbitals.reshape(8, -1, 128), "orb", split_axis=0, concat_axis=0, tiled=True)
    slot, where = tables(pick_place, point_index.reshape(-1, 128))
    blocks = pick(pick_place, slot, where, orbitals, other)
    here = to_y(blocks[2], 2) + to_y(blocks[3], 3) + to_y(blocks[1], 1) + blocks[0]
    here, rows_here = lax.optimization_barrier((here, rows_here))
    around = [to_zh(here, 2), to_zh(here, 3), to_zh(here, 1)]
    pots = pack(place, potentials, other_pot)
    around, pots = lax.optimization_barrier((around, pots))
    here = here + around[0] + around[1] + around[2]
    beside = to_zl(here)
    pair = jnp.stack([here, beside])
    pair, rows_here = lax.optimization_barrier((pair, rows_here))
    rows = [rows_here, to_core(rows_here)]
    pieces = [pair] + [first_axis(pair, d) for d in (2, 3, 1)]
    low, high = join(place, pieces)
    low_up, low_down = second_axis(low, 1), second_axis(low, 3)
    high_up, high_down = second_axis(high, 1), second_axis(high, 3)
    lows = [low, low_up, second_axis(low_up, 1), low_down]
    highs = [high, high_up, second_axis(high_down, 3), high_down]
    each = potentials.shape[0]
    sums = jax.ShapeDtypeStruct((2 * each, 1024), jnp.float32)
    lines = jax.ShapeDtypeStruct((2 * each, 1024), jnp.bfloat16)
    low0, low1, low2, low3 = lows
    high0, high1, high2, high3 = highs
    near = [low0, low1, high0, high3]
    lined, partial, early = call(early_kernel, "early", [lines, sums, sums], 3, place, *rows, *pots, *near)
    partial, early = call(
        middle_kernel, "middle", [sums, sums], 2, place, lined, *pots, early, partial, low3, high1, aliases={5: 0, 4: 1}
    )
    halves = []
    for side, dtype in ((1, jnp.bfloat16), (0, jnp.float32)):
        out = jax.ShapeDtypeStruct((each, 1024), dtype)
        kernel = functools.partial(late_kernel, side)
        halves += call(kernel, "late", [out], 3, place, lined, pots[side], early, partial, *lows, *highs)
    sent, kept = halves
    theirs = to_core(sent)
    blocks = total(place, kept, theirs)
    arrived = [to_owner(blocks[2 * d + dz], d, dz) for d, dz in ORDER[:-1]] + [blocks[0]]
    first = put(ORDER[:4] + ORDER[7:], place, arrived[:4] + arrived[7:])
    return put(ORDER[4:7], place, arrived[4:7], first).reshape(-1, 128)


def solution(mesh):
    return jax.shard_map(
        shards,
        mesh=mesh,
        in_specs=(P("grid", "orb"), P(("grid", "orb"), None), P()),
        out_specs=P("grid", "orb"),
        check_vma=False,
    )
```

```python
import functools

import jax
import jax.numpy as jnp
from jax import lax
from jax.experimental import pallas as pl
from jax.experimental.pallas import tpu as pltpu
from jax.sharding import PartitionSpec as P

NY, NZH, NC, NX, NZL = 4, 4, 2, 4, 2
AXES = ("grid", "orb")
BLOCK = 512
HALF = 256
ORDER = ((2, 1), (0, 1), (2, 0), (3, 1), (1, 1), (3, 0), (1, 0), (0, 0))


def moves(target):
    pairs = []
    for y in range(NY):
        for zh in range(NZH):
            for c in range(NC):
                for x in range(NX):
                    for zl in range(NZL):
                        ty, tzh, tc, tx, tzl = target(y, zh, c, x, zl)
                        src = ((y * NZH + zh) * NC + c) * NX * NZL + x * NZL + zl
                        dst = ((ty % NY * NZH + tzh % NZH) * NC + tc % NC) * NX * NZL + tx % NX * NZL + tzl % NZL
                        pairs.append((src, dst))
    return pairs


def send(value, target):
    return lax.ppermute(value, AXES, moves(target))


def to_core(value):
    return send(value, lambda y, zh, c, x, zl: (y, zh, 1 - c, x, zl))


def to_y(value, d):
    return send(value, lambda y, zh, c, x, zl: (y ^ d, zh, c, x, zl))


def to_zh(value, d):
    return send(value, lambda y, zh, c, x, zl: (y, zh ^ d, c, x, zl))


def to_zl(value):
    return send(value, lambda y, zh, c, x, zl: (y, zh, c, x, 1 - zl))


def first_axis(value, d):
    return send(value, lambda y, zh, c, x, zl: (y ^ (d * c), zh, c, x ^ (d * (1 - c)), zl))


def to_owner(value, d, dz):
    return send(value, lambda y, zh, c, x, zl: (y, zh, c, x ^ d, zl ^ dz))


def second_axis(value, d):
    return send(value, lambda y, zh, c, x, zl: (y + d * (1 - c), zh, c, x + d * c, zl))


def one_hot(places, wanted):
    one, zero = jnp.ones((), jnp.bfloat16), jnp.zeros((), jnp.bfloat16)
    return jnp.where(places == wanted.astype(jnp.int16), one, zero)


def table_kernel(place, index, slot_ref, where_ref):
    slab = place[0]
    idx = index[...]
    lines = idx.shape[0]
    owner = lax.shift_right_logical(idx, 12)
    in_mine = owner == slab
    in_other = owner == (slab ^ 1)
    flags = jnp.concatenate([in_mine.astype(jnp.float32), in_other.astype(jnp.float32)], axis=0)
    upper = (
        (lax.broadcasted_iota(jnp.int32, (128, 128), 0) <= lax.broadcasted_iota(jnp.int32, (128, 128), 1))
        .astype(jnp.float32)
        .astype(jnp.bfloat16)
    )
    counts = jnp.dot(flags.astype(jnp.bfloat16), upper, preferred_element_type=jnp.float32)
    totals = jnp.broadcast_to(counts[:, 127:128], (2 * lines, 128)).astype(jnp.bfloat16)
    to = lax.broadcasted_iota(jnp.int32, (2 * lines, 2 * lines), 0)
    of = lax.broadcasted_iota(jnp.int32, (2 * lines, 2 * lines), 1)
    earlier = ((of < to) & ((of < lines) == (to < lines))).astype(jnp.float32).astype(jnp.bfloat16)
    ranks = counts + jnp.dot(earlier, totals, preferred_element_type=jnp.float32) - 1.0
    slot = jnp.where(in_mine, ranks[:lines], jnp.where(in_other, ranks[lines:] + 256.0, -1.0)).astype(jnp.int32)
    slot_ref[...] = slot
    local = idx & 4095
    high = lax.shift_right_logical(local, 6).astype(jnp.float32)
    low = (local & 63).astype(jnp.float32)
    where = jnp.zeros((BLOCK, 8), jnp.float32)
    rows = lax.broadcasted_iota(jnp.int32, (BLOCK, BLOCK), 0).astype(jnp.int16)
    pick_row = lax.broadcasted_iota(jnp.int32, (8, BLOCK), 0)

    def line(value, b):
        return jnp.concatenate([value[i : i + 1, :] for i in range(4 * b, 4 * b + 4)], axis=1)

    for b in range(8):
        parts = jnp.where(pick_row == 0, line(high, b), jnp.where(pick_row == 1, line(low, b), 0.0))
        where = where + lax.dot_general(
            one_hot(rows, line(slot, b)), parts.astype(jnp.bfloat16), (((1,), (1,)), ((), ())), preferred_element_type=jnp.float32
        )
    where_ref[...] = where


def tables(place, index):
    vmem = pl.BlockSpec(memory_space=pltpu.VMEM)
    return pl.pallas_call(
        table_kernel,
        out_shape=[jax.ShapeDtypeStruct(index.shape, jnp.int32), jax.ShapeDtypeStruct((BLOCK, 8), jnp.float32)],
        in_specs=[pl.BlockSpec(memory_space=pltpu.SMEM), vmem],
        out_specs=[vmem] * 2,
        compiler_params=pltpu.CompilerParams(vmem_limit_bytes=16 * 1024 * 1024),
        cost_estimate=pl.CostEstimate(flops=2_000_000_000, bytes_accessed=2_000_000, transcendentals=0),
        name="tables",
    )(place, index)


def pick_kernel(place, slot_ref, where_ref, mine, other_hbm, *refs):
    outs, other, other_sem = refs[:4], refs[4], refs[5]
    other_copy = pltpu.make_async_copy(other_hbm, other, other_sem)
    other_copy.start()
    half, y = place[1], place[2]
    where = where_ref[...]
    line = (where[:, 0:1] * 64.0 + where[:, 1:2]).astype(jnp.int32)
    picked = []
    wide = 1024
    lane = lax.broadcasted_iota(jnp.int32, (256, wide), 1).astype(jnp.int16)
    for s, block in enumerate((mine, other)):
        if s == 1:
            other_copy.wait()
        want = line[s * 256 : (s + 1) * 256, :]
        total = jnp.zeros((256, 128), jnp.float32)
        for k in range(4096 // wide):
            chosen = one_hot(lane, want - k * wide)
            total = total + jnp.dot(chosen, block[k * wide : (k + 1) * wide, :], preferred_element_type=jnp.float32)
        picked.append(total)
    turned = jnp.concatenate(picked, axis=0).T.astype(jnp.bfloat16)
    rows = lax.broadcasted_iota(jnp.int32, (BLOCK, BLOCK), 0).astype(jnp.int16)
    for d in range(4):
        b = half * 4 + (y ^ d)
        four = slot_ref[pl.ds(b * 4, 4), :]
        row = jnp.concatenate([four[i : i + 1, :] for i in range(4)], axis=1)
        values = jnp.dot(turned, one_hot(rows, row), preferred_element_type=jnp.float32).astype(jnp.bfloat16)
        outs[d][0] = values[:, :HALF]
        outs[d][1] = values[:, HALF:]


def pick(place, slot, where, mine, other):
    block = jax.ShapeDtypeStruct((2, 128, HALF), jnp.bfloat16)
    vmem = pl.BlockSpec(memory_space=pltpu.VMEM)
    return pl.pallas_call(
        pick_kernel,
        out_shape=[block] * 4,
        in_specs=[pl.BlockSpec(memory_space=pltpu.SMEM), vmem, vmem, vmem, pl.BlockSpec(memory_space=pl.ANY)],
        out_specs=[vmem] * 4,
        scratch_shapes=[pltpu.VMEM(other.shape, other.dtype), pltpu.SemaphoreType.DMA],
        compiler_params=pltpu.CompilerParams(vmem_limit_bytes=16 * 1024 * 1024),
        cost_estimate=pl.CostEstimate(flops=2_500_000_000, bytes_accessed=4_000_000, transcendentals=0),
        name="pick",
    )(place, slot, where, mine, other)


def join_kernel(place, *refs):
    pieces, messages = (refs[0], refs[3], refs[1], refs[2]), refs[4:6]
    core = place[2]
    for c in range(2):

        @pl.when(core == c)
        def _():
            for d in range(4):
                for dz in range(2):
                    for half in range(2):
                        value = pieces[d][dz, half]
                        if c == 0:
                            messages[half][d, dz] = value
                        else:
                            messages[d // 2][d % 2 * 2 + half, dz] = value


def join(place, pieces):
    vmem = pl.BlockSpec(memory_space=pltpu.VMEM)
    message = jax.ShapeDtypeStruct((4, 2, 128, HALF), jnp.bfloat16)
    return pl.pallas_call(
        join_kernel,
        out_shape=[message] * 2,
        in_specs=[pl.BlockSpec(memory_space=pltpu.SMEM)] + [vmem] * 4,
        out_specs=[vmem] * 2,
        compiler_params=pltpu.CompilerParams(vmem_limit_bytes=16 * 1024 * 1024),
        cost_estimate=pl.CostEstimate(flops=0, bytes_accessed=2_000_000, transcendentals=0),
        name="join",
    )(place, *pieces)


def pack_kernel(place, *refs):
    core = place[2]
    sources, outs, sem = refs[:2], refs[2:4], refs[4]
    copies = []
    for s in range(2):
        for b in range(8):
            lanes = pl.ds(pl.multiple_of((core * 8 + b) * HALF, HALF), HALF)
            copies.append(pltpu.make_async_copy(sources[s].at[:, lanes], outs[s].at[b], sem.at[s, b]))
    for copy in copies:
        copy.start()
    for copy in copies:
        copy.wait()


def pack(place, mine, theirs):
    anyspace = pl.BlockSpec(memory_space=pl.ANY)
    return pl.pallas_call(
        pack_kernel,
        out_shape=[jax.ShapeDtypeStruct((8, mine.shape[0], HALF), jnp.bfloat16)] * 2,
        in_specs=[pl.BlockSpec(memory_space=pltpu.SMEM), anyspace, anyspace],
        out_specs=[pl.BlockSpec(memory_space=pltpu.VMEM)] * 2,
        scratch_shapes=[pltpu.SemaphoreType.DMA((2, 8))],
        compiler_params=pltpu.CompilerParams(vmem_limit_bytes=16 * 1024 * 1024),
        cost_estimate=pl.CostEstimate(flops=0, bytes_accessed=8_000_000, transcendentals=0),
        name="pack",
    )(place, mine, theirs)


def low_block(core, y, e):
    return jnp.where(core == 0, ((y - e) & 3) * 2, (y ^ (e // 2)) * 2 + e % 2)


def high_block(core, y, e):
    return jnp.where(core == 0, ((y - e) & 3) * 2 + 1, (y ^ (2 + e // 2)) * 2 + e % 2)


def flat(message):
    return message[...].reshape(1024, HALF)


def square(message, k):
    return message[k].reshape(HALF, HALF)


def weigh(pots, block, density):
    each = density.shape[0] // len(pots)
    parts = [
        pot[block].astype(jnp.float32) * density[s * each : (s + 1) * each] for s, pot in enumerate(pots)
    ]
    return jnp.concatenate(parts, axis=0).astype(jnp.bfloat16)


def times(left, right):
    return jnp.dot(left, right, preferred_element_type=jnp.float32)


def spread(weighted, parts):
    return lax.dot_general(
        weighted, jnp.concatenate(parts, axis=1), (((1,), (1,)), ((), ())), preferred_element_type=jnp.float32
    )


def column_lanes(n):
    return slice(n * HALF, (n + 1) * HALF)


def whole_chunks(rows, pots, chunks, scratch):
    for k, (message, block) in enumerate(chunks):
        scratch[:, column_lanes(k)] = weigh(pots, block, times(rows[...], flat(message)))
    for n in range(4):
        yield n, spread(scratch[:, : len(chunks) * HALF], [square(message, n) for message, _ in chunks])


def early_kernel(
    place, mine, theirs, pot_mine, pot_theirs, low0, high0, rows, partial, out, scratch
):
    x, y, core, zl = place[0], place[1], place[2], place[3]
    each = mine.shape[1]
    pots = (pot_mine, pot_theirs)
    for k in range(8):
        block = jnp.where(core == 0, x ^ (k // 2), (x - k // 2) & 3) * 2 + (zl ^ (k % 2))
        lanes = slice(k * 128, (k + 1) * 128)
        rows[:each, lanes] = mine[block]
        rows[each:, lanes] = theirs[block]

    @pl.when(core == 0)
    def _():
        chunks = [(low0, low_block(core, y, 0)), (high0, high_block(core, y, 0))]
        for n, total in whole_chunks(rows, pots, chunks, scratch):
            out[:, column_lanes(n)] = total

    @pl.when(core == 1)
    def _():
        for k in range(4):
            out[:, column_lanes(k)] = times(rows[:, column_lanes(0)], square(low0, k))
            partial[:, column_lanes(k)] = times(rows[:, column_lanes(0)], square(high0, k))


def middle_kernel(
    a, b, place, rows, pot_mine, pot_theirs, low_before, high_before, low, high, partial, out, scratch
):
    y, core = place[1], place[2]

    @pl.when(core == 0)
    def _():
        chunks = [(low, low_block(core, y, a)), (high, high_block(core, y, b))]
        for n, total in whole_chunks(rows, (pot_mine, pot_theirs), chunks, scratch):
            out[:, column_lanes(n)] = low_before[:, column_lanes(n)] + total

    @pl.when(core == 1)
    def _():
        for k in range(4):
            lanes = column_lanes(k)
            out[:, lanes] = low_before[:, lanes] + times(rows[:, column_lanes(a)], square(low, k))
            partial[:, lanes] = high_before[:, lanes] + times(rows[:, column_lanes(b)], square(high, k))


def late_kernel(side, place, rows, pot, before, partial, *refs):
    lows, highs, (out, scratch) = refs[:4], refs[4:8], refs[8:]
    y, core = place[1], place[2]
    each = out.shape[0]
    part = slice(side * each, (side + 1) * each)

    @pl.when(core == 0)
    def _():
        chunks = [(lows[2], low_block(core, y, 2)), (highs[2], high_block(core, y, 2))]
        for n, total in whole_chunks(rows.at[part], (pot,), chunks, scratch):
            out[:, column_lanes(n)] = (before[part, column_lanes(n)] + total).astype(out.dtype)

    @pl.when(core == 1)
    def _():
        for i, (known, messages, where) in enumerate(((before, lows, low_block), (partial, highs, high_block))):
            for k in range(4):
                density = known[part, column_lanes(k)] + times(rows[part, column_lanes(2)], square(messages[2], k))
                scratch[:, column_lanes(4 * i + k)] = weigh((pot,), where(core, y, k), density)
        for n in range(4):
            parts = [square(lows[n], k) for k in range(4)] + [square(highs[n], k) for k in range(4)]
            out[:, column_lanes(n)] = spread(scratch[...], parts).astype(out.dtype)


def call(kernel, name, outs, work, *operands, aliases=None):
    vmem = pl.BlockSpec(memory_space=pltpu.VMEM)
    lines = outs[-1].shape[0]
    return pl.pallas_call(
        kernel,
        out_shape=outs,
        in_specs=[pl.BlockSpec(memory_space=pltpu.SMEM)] + [vmem] * (len(operands) - 1),
        out_specs=[vmem] * len(outs),
        scratch_shapes=[pltpu.VMEM((lines, 2048), jnp.bfloat16)],
        input_output_aliases=aliases or {},
        compiler_params=pltpu.CompilerParams(vmem_limit_bytes=16 * 1024 * 1024),
        cost_estimate=pl.CostEstimate(
            flops=work * lines * 1024 * 1024, bytes_accessed=4 * 1024 * 1024, transcendentals=0
        ),
        name=name,
    )(*operands)


def total_kernel(place, mine, theirs, *outs):
    x, core = place[0], place[2]
    for d in range(4):
        other = (x - (x ^ d)) & 3
        here, there = jnp.where(core == 0, d, other), jnp.where(core == 0, other, d)
        for dz in range(2):
            value = mine[:, pl.ds(pl.multiple_of(here * 256 + dz * 128, 128), 128)]
            value = value + theirs[:, pl.ds(pl.multiple_of(there * 256 + dz * 128, 128), 128)].astype(jnp.float32)
            outs[2 * d + dz][...] = (-value).astype(jnp.bfloat16)


def total(place, mine, theirs):
    vmem = pl.BlockSpec(memory_space=pltpu.VMEM)
    return pl.pallas_call(
        total_kernel,
        out_shape=[jax.ShapeDtypeStruct((mine.shape[0], 128), jnp.bfloat16)] * 8,
        in_specs=[pl.BlockSpec(memory_space=pltpu.SMEM), vmem, vmem],
        out_specs=[vmem] * 8,
        compiler_params=pltpu.CompilerParams(vmem_limit_bytes=16 * 1024 * 1024),
        name="total",
    )(place, mine, theirs)


def put_kernel(order, place, *refs):
    blocks, out, sem = refs[: len(order)], refs[-2], refs[-1]
    x, zl = place[0], place[3]
    copies = []
    for i, (d, dz) in enumerate(order):
        run = (x ^ d) * 2 + (zl ^ dz)
        copies.append(pltpu.make_async_copy(blocks[i], out.at[run], sem.at[i]))
    for copy in copies:
        copy.start()
    for copy in copies:
        copy.wait()


def put(order, place, blocks, before=None):
    vmem = pl.BlockSpec(memory_space=pltpu.VMEM)
    anyspace = pl.BlockSpec(memory_space=pl.ANY)
    number = len(order)
    return pl.pallas_call(
        functools.partial(put_kernel, order),
        out_shape=jax.ShapeDtypeStruct((8,) + blocks[0].shape, jnp.bfloat16),
        in_specs=[pl.BlockSpec(memory_space=pltpu.SMEM)] + [vmem] * number + [anyspace] * (before is not None),
        out_specs=anyspace,
        scratch_shapes=[pltpu.SemaphoreType.DMA((number,))],
        input_output_aliases={} if before is None else {number + 1: 0},
        compiler_params=pltpu.CompilerParams(vmem_limit_bytes=16 * 1024 * 1024),
        cost_estimate=pl.CostEstimate(flops=0, bytes_accessed=number * 300_000, transcendentals=0),
        name="put",
    )(place, *blocks, *([] if before is None else [before]))


def shards(orbitals, potentials, point_index):
    grid, orb = lax.axis_index("grid"), lax.axis_index("orb")
    c = lax.rem(grid, NC)
    y = lax.div(grid, NZH * NC)
    x, zl = lax.div(orb, NZL), lax.rem(orb, NZL)
    pick_place = jnp.stack([grid, c, y]).astype(jnp.int32)
    place = jnp.stack([x, y, c, zl]).astype(jnp.int32)

    other = to_core(orbitals)
    other_pot = to_core(potentials)
    rows_here = lax.all_to_all(orbitals.reshape(8, -1, 128), "orb", split_axis=0, concat_axis=0, tiled=True)
    slot, where = tables(pick_place, point_index.reshape(-1, 128))
    blocks = pick(pick_place, slot, where, orbitals, other)
    here = to_y(blocks[2], 2) + to_y(blocks[3], 3) + to_y(blocks[1], 1) + blocks[0]
    here, rows_here = lax.optimization_barrier((here, rows_here))
    around = [to_zh(here, 2), to_zh(here, 3), to_zh(here, 1)]
    pots = pack(place, potentials, other_pot)
    around, pots = lax.optimization_barrier((around, pots))
    here = here + around[0] + around[1] + around[2]
    beside = to_zl(here)
    pair = jnp.stack([here, beside])
    pair, rows_here = lax.optimization_barrier((pair, rows_here))
    rows = [rows_here, to_core(rows_here)]
    pieces = [pair] + [first_axis(pair, d) for d in (2, 3, 1)]
    low, high = join(place, pieces)
    low_up, low_down = second_axis(low, 1), second_axis(low, 3)
    high_up, high_down = second_axis(high, 1), second_axis(high, 3)
    lows = [low, low_up, second_axis(low_up, 1), low_down]
    highs = [high, high_up, second_axis(high_down, 3), high_down]
    each = potentials.shape[0]
    sums = jax.ShapeDtypeStruct((2 * each, 1024), jnp.float32)
    lines = jax.ShapeDtypeStruct((2 * each, 1024), jnp.bfloat16)
    low0, low1, low2, low3 = lows
    high0, high1, high2, high3 = highs
    lined, partial, early = call(early_kernel, "early", [lines, sums, sums], 2, place, *rows, *pots, low0, high0)
    for a, b in ((1, 3), (3, 1)):
        kernel = functools.partial(middle_kernel, a, b)
        args = [place, lined, *pots, early, partial, lows[a], highs[b]]
        partial, early = call(kernel, "middle", [sums, sums], 2, *args, aliases={5: 0, 4: 1})
    halves = []
    for side, dtype in ((1, jnp.bfloat16), (0, jnp.float32)):
        out = jax.ShapeDtypeStruct((each, 1024), dtype)
        kernel = functools.partial(late_kernel, side)
        halves += call(kernel, "late", [out], 3, place, lined, pots[side], early, partial, *lows, *highs)
    sent, kept = halves
    theirs = to_core(sent)
    blocks = total(place, kept, theirs)
    arrived = [to_owner(blocks[2 * d + dz], d, dz) for d, dz in ORDER[:-1]] + [blocks[0]]
    first = put(ORDER[:4] + ORDER[7:], place, arrived[:4] + arrived[7:])
    return put(ORDER[4:7], place, arrived[4:7], first).reshape(-1, 128)


def solution(mesh):
    return jax.shard_map(
        shards,
        mesh=mesh,
        in_specs=(P("grid", "orb"), P(("grid", "orb"), None), P()),
        out_specs=P("grid", "orb"),
        check_vma=False,
    )
```
